32 devices in a mesh: shard: 8 (over z, y), rep: 4 (over x, core).
Axes of the slice: x: 2, y: 2, z: 4, core: 2. Of those that a mesh axis runs over, the one named last changes fastest.
Arguments:
- node_feat: bfloat16 [256, 128, 256], P(('shard', 'rep'))
- node_cot: bfloat16 [256, 128, 256], P(('shard', 'rep'))
- edge_length: float32 [256, 1536], P(('shard', 'rep')), may hold values from 0.5 to 5.5
- atom_count: int32 [256], P(('shard', 'rep')), may hold values from 32 to 128, as said below
- edge_count: int32 [256], P(('shard', 'rep')), may hold values from 384 to 1536, as said below
- edge_source: int32 [256, 1536], P(('shard', 'rep')), may hold values from 0 to 127, as said below
- edge_target: int32 [256, 1536], P(('shard', 'rep')), may hold values from 0 to 127, as said below
- dataset_tag: int32 [256], P(('shard', 'rep')), may hold values from 0 to 1
- charge_tag: int32 [256], P(('shard', 'rep')), may hold values from 0 to 1
- spin_tag: int32 [256], P(('shard', 'rep')), may hold values from 0 to 1
- dataset_gain: float32 [2, 32], replicated, may hold values from 0.2 to 5
- charge_gain: float32 [2, 32], replicated, may hold values from 0.2 to 5
- spin_gain: float32 [2, 32], replicated, may hold values from 0.2 to 5
- params: float32 [32, 128, 2, 128], P(None, 'shard'), may hold values from -0.375 to 0.375
- moment_one: float32 [32, 128, 2, 128], P(None, 'shard'), may hold values from -0.9 to 0.9
- moment_two: float32 [32, 128, 2, 128], P(None, 'shard'), may hold values from 0.0001 to 0.01
Outputs:
- new_params: float32 [32, 128, 2, 128], P(None, 'shard')
- new_moment_one: float32 [32, 128, 2, 128], P(None, 'shard')
- new_moment_two: float32 [32, 128, 2, 128], P(None, 'shard')
- full_weights: bfloat16 [32, 128, 2, 128], replicated
The draws below stay inside these ranges and needn't reach their ends.
Inputs may be any that keep to these rules, and one draw needn't show every extreme that they name: `atom_count`: every system has at least a quarter of its atom slots filled. `edge_count`: every system has at least a quarter of its edge slots live. `edge_source`: every slot, live or not, names an atom below its system's atom count. `edge_target`: every slot, live or not, names an atom below its system's atom count.
All inputs are finite; a program needn't handle non-finite values.
Results may differ from the reference program's by a relative error of at most 0.0036.
Values may be sent and summed in bfloat16 or wider, within the bound.
A program may use at most 64 MiB of HBM per device.

```python
import math
import jax
import jax.numpy as jnp
from jax import lax

CH = 128
EXPERTS = 32
DATASETS = 2
CHARGES = 2
SPINS = 2
ATOMS = 128
EDGE_SLOTS = 1536
STEP = 10
SYS_DEV = 8
SYSTEMS = 256


def system_atoms(key):
    counts_key = jax.random.fold_in(key, 101)
    counts = jax.random.randint(counts_key, (SYSTEMS,), ATOMS // 4, ATOMS + 1)
    counts = counts.at[::SYS_DEV].set(ATOMS)
    return counts.astype(jnp.int32)


def edge_atoms(key, salt):
    counts = system_atoms(key)
    raw_key = jax.random.fold_in(key, salt)
    raw_draw = jax.random.randint(raw_key, (SYSTEMS, EDGE_SLOTS), 0, 1073741824)
    chosen = raw_draw % counts[:, None]
    chosen = chosen.at[::SYS_DEV, 0].set(ATOMS - 1)
    return chosen.astype(jnp.int32)


def draw_atom_count(key, part):
    return system_atoms(key)


def draw_edge_count(key, part):
    count_key = jax.random.fold_in(key, 202)
    counts = jax.random.randint(count_key, (SYSTEMS,), EDGE_SLOTS // 4, EDGE_SLOTS + 1)
    counts = counts.at[::SYS_DEV].set(EDGE_SLOTS)
    return counts.astype(jnp.int32)


def draw_edge_source(key, part):
    return edge_atoms(key, 303)


def draw_edge_target(key, part):
    return edge_atoms(key, 404)


def draw_node_feat(key, part):
    value_key = jax.random.fold_in(key, 505)
    row_key = jax.random.fold_in(key, 606)
    column_key = jax.random.fold_in(key, 707)
    pattern_key = jax.random.fold_in(key, 808)
    shared_key = jax.random.fold_in(key, 909)
    sign_key = jax.random.fold_in(key, 1010)
    channel = jnp.arange(2 * CH) % CH
    trend = channel.astype(jnp.float32) / float(max(CH - 1, 1))
    column_draw = jax.random.uniform(column_key, (CH,), jnp.float32)
    column_scale = 10.0 ** (0.5 * trend + 0.5 * column_draw[channel])
    row_scale = 10.0 ** jax.random.uniform(row_key, (SYSTEMS, ATOMS, 1), jnp.float32)
    pattern = jax.random.normal(pattern_key, (1, 1, 2 * CH), jnp.float32)
    shared = jax.random.normal(shared_key, (1, 1, 2 * CH), jnp.float32)
    signs = (jax.random.randint(sign_key, (SYSTEMS, 1, 1), 0, 2) * 2 - 1).astype(jnp.float32)
    shared_weight = float(SYSTEMS) ** (-0.5)
    base = jax.random.normal(value_key, (SYSTEMS, ATOMS, 2 * CH), jnp.float32)
    offset = 0.8 * (signs * pattern + shared_weight * shared)
    return ((base + offset) * column_scale[None, None, :] * row_scale).astype(jnp.bfloat16)


def draw_node_cot(key, part):
    value_key = jax.random.fold_in(key, 1111)
    mean_key = jax.random.fold_in(key, 1212)
    column_mean = jax.random.normal(mean_key, (1, 1, 2 * CH), jnp.float32)
    base = jax.random.normal(value_key, (SYSTEMS, ATOMS, 2 * CH), jnp.float32)
    values = base + 0.3 * column_mean
    return jnp.clip(values, -6.0, 6.0).astype(jnp.bfloat16)


def touch_ends(result, own_key, smallest, largest):
    spot = [jax.random.randint(jax.random.fold_in(own_key, axis), (), 0, length) for axis, length in enumerate(result.shape)]
    main_axis = result.shape.index(max(result.shape))
    neighbour = spot[:main_axis] + [(spot[main_axis] + 1) % result.shape[main_axis]] + spot[main_axis + 1:]
    return result.at[tuple(spot)].set(smallest).at[tuple(neighbour)].set(largest)


def level_of(key, shape, shards, least, high):
    factor_of = 1.0
    for axis_at, shards_of in shards:
        draws = jax.random.uniform(jax.random.fold_in(jax.random.fold_in(key, 6), axis_at), (shards_of,), jnp.float32, least / len(shards), high / len(shards))
        factor_of = factor_of * jnp.repeat(jnp.exp(draws), shape[axis_at] // shards_of).reshape((-1,) + (1,) * (len(shape) - 1 - axis_at))
    return factor_of


def centred(stream_key, extent, scale, bound, pieces=(), held_as=jnp.bfloat16):
    drawn = jax.random.normal(stream_key, extent, jnp.float32) * scale
    if len(pieces) > 0:
        drawn = level_of(stream_key, extent, pieces, -0.22, 0.18) * drawn
    return jnp.clip(drawn, min=-bound, max=bound).astype(held_as)


def setup_inputs(seed: int = 0) -> dict:
    splits = jax.random.split(jax.random.key(seed), 17)
    node_feat = draw_node_feat(jax.random.fold_in(splits[16], 71), 0)
    node_cot = draw_node_cot(jax.random.fold_in(splits[16], 71), 0)
    edge_length = jnp.clip(0.5 + 5.0 * jax.random.uniform(splits[2], (SYSTEMS, EDGE_SLOTS), jnp.float32) ** level_of(splits[2], (SYSTEMS, EDGE_SLOTS), ((0, 32),), -0.2, 0.2), 0.5, 5.5)
    atom_count = draw_atom_count(jax.random.fold_in(splits[16], 71), 0)
    edge_count = draw_edge_count(jax.random.fold_in(splits[16], 71), 0)
    edge_source = draw_edge_source(jax.random.fold_in(splits[16], 71), 0)
    edge_target = draw_edge_target(jax.random.fold_in(splits[16], 71), 0)
    dataset_tag = touch_ends(jax.random.randint(splits[7], (SYSTEMS,), 0, DATASETS), jax.random.fold_in(splits[7], 1), 0, DATASETS - 1).astype(jnp.int32)
    charge_tag = touch_ends(jax.random.randint(splits[8], (SYSTEMS,), 0, CHARGES), jax.random.fold_in(splits[8], 1), 0, CHARGES - 1).astype(jnp.int32)
    spin_tag = touch_ends(jax.random.randint(splits[9], (SYSTEMS,), 0, SPINS), jax.random.fold_in(splits[9], 1), 0, SPINS - 1).astype(jnp.int32)
    dataset_gain = jnp.clip(jnp.exp(jax.random.uniform(splits[10], (DATASETS, EXPERTS), jnp.float32, math.log(0.2), math.log(5.0))), 0.2, 5.0)
    charge_gain = jnp.clip(jnp.exp(jax.random.uniform(splits[11], (CHARGES, EXPERTS), jnp.float32, math.log(0.2), math.log(5.0))), 0.2, 5.0)
    spin_gain = jnp.clip(jnp.exp(jax.random.uniform(splits[12], (SPINS, EXPERTS), jnp.float32, math.log(0.2), math.log(5.0))), 0.2, 5.0)
    params = centred(splits[13], (EXPERTS, CH, 2, CH), (2 * CH) ** -0.5, 0.375, ((1, 8),), jnp.float32)
    moment_one = centred(splits[14], (EXPERTS, CH, 2, CH), 0.15, 0.9, ((1, 8),), jnp.float32)
    moment_two = jnp.clip(jnp.exp(math.log(0.01) - 4.6051702 * jax.random.uniform(splits[15], (EXPERTS, CH, 2, CH), jnp.float32) ** level_of(splits[15], (EXPERTS, CH, 2, CH), ((1, 8),), -0.2, 0.2)), 0.0001, 0.01)
    return {"node_feat": node_feat, "node_cot": node_cot, "edge_length": edge_length, "atom_count": atom_count, "edge_count": edge_count, "edge_source": edge_source, "edge_target": edge_target, "dataset_tag": dataset_tag, "charge_tag": charge_tag, "spin_tag": spin_tag, "dataset_gain": dataset_gain, "charge_gain": charge_gain, "spin_gain": spin_gain, "params": params, "moment_one": moment_one, "moment_two": moment_two}


beta_one = 0.9
beta_two = 0.999
adam_eps = 1e-08
learn_rate = 0.01
decay_rate = 0.01
cutoff_radius = 6.0

def envelope(length):
    ratio = length / cutoff_radius
    return 1.0 - 21.0 * ratio ** 5 + 35.0 * ratio ** 6 - 15.0 * ratio ** 7

def pick_rows(node_rows, slot_ids):
    return node_rows[slot_ids]

def mixing_table(dataset_gain, charge_gain, spin_gain):
    product_table = dataset_gain[:, None, None, :] * charge_gain[None, :, None, :] * spin_gain[None, None, :, :]
    product_table = product_table.reshape(-1, product_table.shape[-1])
    return product_table / lax.optimization_barrier(jnp.sum(product_table, axis=1, keepdims=True))

def onehot_rows(dataset_tag, charge_tag, spin_tag, charge_count, spin_count, row_total):
    tag_rows = (dataset_tag * charge_count + charge_tag) * spin_count + spin_tag
    return (tag_rows[:, None] == jnp.arange(row_total, dtype=jnp.int32)[None, :]).astype(jnp.float32)

def edge_cotangent(node_cot, edge_target, edge_count, atom_count, atom_slots):
    picked = jax.vmap(pick_rows)(node_cot, edge_target)
    slot_index = lax.broadcasted_iota(jnp.int32, edge_target.shape, 1)
    live_mask = (slot_index < edge_count[:, None]).astype(jnp.float32)
    atom_weight = float(atom_slots) / atom_count.astype(jnp.float32)
    factor = live_mask * atom_weight[:, None]
    return (picked.astype(jnp.float32) * factor[:, :, None]).astype(jnp.bfloat16)

def adam_update(gradients, params, moment_one, moment_two, square_sum, norm_limit):
    clip_factor = jnp.minimum(1.0, norm_limit / (jnp.sqrt(square_sum) + 1e-06))
    clipped = clip_factor * gradients
    new_one = beta_one * moment_one + (1.0 - beta_one) * clipped
    new_two = beta_two * moment_two + (1.0 - beta_two) * clipped * clipped
    first_fix = 1.0 - beta_one ** STEP
    second_fix = 1.0 - beta_two ** STEP
    direction = new_one / first_fix / (jnp.sqrt(new_two / second_fix) + adam_eps)
    new_params = params - learn_rate * (direction + decay_rate * params)
    return (new_params, new_one, new_two)

def reference(node_feat, node_cot, edge_length, atom_count, edge_count, edge_source, edge_target, dataset_tag, charge_tag, spin_tag, dataset_gain, charge_gain, spin_gain, params, moment_one, moment_two):
    mixing = mixing_table(dataset_gain, charge_gain, spin_gain)
    row_total = DATASETS * CHARGES * SPINS
    tag_onehot = onehot_rows(dataset_tag, charge_tag, spin_tag, CHARGES, SPINS, row_total)
    block_count = SYSTEMS // SYS_DEV

    def by_block(array):
        return array.reshape((block_count, SYS_DEV) + array.shape[1:])

    def scan_step(running, block_items):
        feat_block, cot_block, length_block, atoms_block, edges_block, source_block, target_block, onehot_block = block_items
        edge_grad = edge_cotangent(cot_block, target_block, edges_block, atoms_block, ATOMS)
        picked = jax.vmap(pick_rows)(feat_block, source_block)
        edge_input = (picked.astype(jnp.float32) * envelope(length_block)[:, :, None]).astype(jnp.bfloat16)
        products = jnp.einsum('sja,sjb->sab', edge_input.astype(jnp.float32), edge_grad.astype(jnp.float32), precision=lax.Precision.HIGHEST)
        real_part = products[:, :CH, :CH] + products[:, CH:, CH:]
        imag_part = products[:, :CH, CH:] - products[:, CH:, :CH]
        system_grad = jnp.stack([real_part, imag_part], axis=2)
        added = jnp.einsum('sk,scto->ckto', onehot_block, system_grad, precision=lax.Precision.HIGHEST)
        return (running + added, None)
    initial = jnp.zeros((CH, row_total, 2, CH), jnp.float32)
    blocks = tuple((by_block(array) for array in (node_feat, node_cot, edge_length, atom_count, edge_count, edge_source, edge_target, tag_onehot)))
    grouped, _ = lax.scan(scan_step, initial, blocks)
    gradients = jnp.einsum('ke,ckto->ecto', mixing, grouped, precision=lax.Precision.HIGHEST)
    square_sum = jnp.sum(gradients * gradients)
    norm_limit = math.sqrt(EXPERTS * 2 * CH * CH)
    new_params, new_one, new_two = adam_update(gradients, params, moment_one, moment_two, square_sum, norm_limit)
    return (new_params, new_one, new_two, new_params.astype(jnp.bfloat16))
```

```python
import functools
import math

import jax
import jax.numpy as jnp
from jax import lax
from jax.experimental import pallas as pl
from jax.experimental.pallas import tpu as pltpu
from jax.sharding import PartitionSpec as P

STEP = 10


beta_one = 0.9
beta_two = 0.999
adam_eps = 1e-08
learn_rate = 0.01
decay_rate = 0.01
cutoff_radius = 6.0


def envelope(length):
    ratio = length / cutoff_radius
    return 1.0 - 21.0 * ratio**5 + 35.0 * ratio**6 - 15.0 * ratio**7


def mixing_table(dataset_gain, charge_gain, spin_gain):
    product_table = (
        dataset_gain[:, None, None, :] * charge_gain[None, :, None, :] * spin_gain[None, None, :, :]
    )
    product_table = product_table.reshape(-1, product_table.shape[-1])
    return product_table / jnp.sum(product_table, axis=1, keepdims=True)


def onehot_rows(dataset_tag, charge_tag, spin_tag, charge_count, spin_count, row_total):
    tag_rows = (dataset_tag * charge_count + charge_tag) * spin_count + spin_tag
    return (tag_rows[:, None] == jnp.arange(row_total, dtype=jnp.int32)[None, :]).astype(
        jnp.float32
    )


def select_rows(node_rows, slot_ids):
    atom_ids = lax.broadcasted_iota(jnp.int32, (1, node_rows.shape[0]), 1)
    selector = (slot_ids[:, None] == atom_ids).astype(jnp.bfloat16)
    return jnp.dot(selector, node_rows, preferred_element_type=jnp.float32)


def system_product(items):
    feat_rows, cot_rows, length_row, atoms_here, edges_here, source_row, target_row = items
    atom_slots = feat_rows.shape[0]
    edge_input = (select_rows(feat_rows, source_row) * envelope(length_row)[:, None]).astype(
        jnp.bfloat16
    )
    slot_index = lax.broadcasted_iota(jnp.int32, source_row.shape, 0)
    live_mask = (slot_index < edges_here).astype(jnp.float32)
    factor = live_mask * (float(atom_slots) / atoms_here.astype(jnp.float32))
    edge_grad = (select_rows(cot_rows, target_row) * factor[:, None]).astype(jnp.bfloat16)
    return lax.dot_general(
        edge_input, edge_grad, (((0,), (0,)), ((), ())), preferred_element_type=jnp.float32
    )


def adam_update(gradients, params, moment_one, moment_two, square_sum, norm_limit):
    clip_factor = jnp.minimum(1.0, norm_limit / (jnp.sqrt(square_sum) + 1e-06))
    clipped = clip_factor * gradients
    new_one = beta_one * moment_one + (1.0 - beta_one) * clipped
    new_two = beta_two * moment_two + (1.0 - beta_two) * clipped * clipped
    first_fix = 1.0 - beta_one**STEP
    second_fix = 1.0 - beta_two**STEP
    direction = new_one / first_fix / (jnp.sqrt(new_two / second_fix) + adam_eps)
    new_params = params - learn_rate * (direction + decay_rate * params)
    return (new_params, new_one, new_two)


def plain_local(
    node_feat,
    node_cot,
    edge_length,
    atom_count,
    edge_count,
    edge_source,
    edge_target,
    dataset_tag,
    charge_tag,
    spin_tag,
    dataset_gain,
    charge_gain,
    spin_gain,
    params,
    moment_one,
    moment_two,
):
    channels = node_feat.shape[2] // 2
    mixing = mixing_table(dataset_gain, charge_gain, spin_gain)
    tag_onehot = onehot_rows(
        dataset_tag, charge_tag, spin_tag, charge_gain.shape[0], spin_gain.shape[0], mixing.shape[0]
    )
    products = lax.map(
        system_product,
        (node_feat, node_cot, edge_length, atom_count, edge_count, edge_source, edge_target),
    )
    real_part = products[:, :channels, :channels] + products[:, channels:, channels:]
    imag_part = products[:, :channels, channels:] - products[:, channels:, :channels]
    system_grad = jnp.stack([real_part, imag_part], axis=2)
    local_term = jnp.einsum(
        "sk,scto->ckto", tag_onehot, system_grad, precision=lax.Precision.HIGHEST
    )
    summed = lax.psum_scatter(local_term, "shard", scatter_dimension=0, tiled=True)
    summed = lax.psum(summed, "rep")
    gradients = jnp.einsum("ke,ckto->ecto", mixing, summed, precision=lax.Precision.HIGHEST)
    square_sum = lax.psum(jnp.sum(gradients * gradients), "shard")
    norm_limit = math.sqrt(mixing.shape[1] * 2 * channels * channels)
    new_params, new_one, new_two = adam_update(
        gradients, params, moment_one, moment_two, square_sum, norm_limit
    )
    full_weights = lax.all_gather(new_params.astype(jnp.bfloat16), "shard", axis=1, tiled=True)
    return (new_params, new_one, new_two, full_weights)


MIB = 1024 * 1024
MESH = pl.DeviceIdType.MESH


def split_dot(left, right, contract):
    high = right.astype(jnp.bfloat16)
    low = (right - high.astype(jnp.float32)).astype(jnp.bfloat16)
    dims = (contract, ((), ()))
    return lax.dot_general(
        left, high, dims, preferred_element_type=jnp.float32
    ) + lax.dot_general(left, low, dims, preferred_element_type=jnp.float32)


def partial_kernel(
    charge_count, spin_count, reps, feat, cot, length, atoms, edges, source, target,
    dataset, charge, spin, pieces, grouped,
):
    systems, slots, width = feat.shape
    channels = width // 2
    lanes = source.shape[1]
    grouped[...] = jnp.zeros_like(grouped)
    weight = envelope(length[...])
    slot_index = lax.broadcasted_iota(jnp.int32, (1, lanes), 1)
    atom_index = lax.broadcasted_iota(jnp.int32, (slots, lanes), 0)
    for s in range(systems):
        count = jnp.full((1, lanes), atoms[s], jnp.int32).astype(jnp.float32)
        factor = jnp.where(slot_index < edges[s], float(slots) / count, 0.0)
        row = weight[s : s + 1, :] * factor
        left = jnp.where(atom_index == source[s : s + 1, :], row, 0.0).astype(jnp.bfloat16)
        right = jnp.where(atom_index == target[s : s + 1, :], 1.0, 0.0).astype(jnp.bfloat16)
        pairs = lax.dot_general(
            right, left, (((1,), (1,)), ((), ())), preferred_element_type=jnp.float32
        )
        mixed = split_dot_left(pairs, cot[s])
        real, imag = mixed[:, :channels], mixed[:, channels:]
        block = jnp.concatenate(
            [
                jnp.concatenate([real, imag], axis=1),
                jnp.concatenate([imag, -real], axis=1),
            ],
            axis=0,
        )
        rows = feat[s]
        stacked = jnp.concatenate([rows[:, :channels], rows[:, channels:]], axis=0)
        product = split_dot(stacked, block, ((0,), (0,)))
        tag = (dataset[s] * charge_count + charge[s]) * spin_count + spin[s]
        grouped[tag, pl.ds(0, channels, stride=2), :] += product[:, :channels]
        grouped[tag, pl.ds(1, channels, stride=2), :] += product[:, channels:]
    tags = grouped.shape[0]
    shards = pieces.shape[2]
    for s in range(shards):
        for r in range(reps):
            at = (s * reps + r) * 8
            pieces[r % 2, r // 2, s] = (
                grouped[:, at : at + 8, :].reshape(tags * 8, channels).astype(jnp.bfloat16)
            )


def split_dot_left(left, right):
    high = left.astype(jnp.bfloat16)
    low = (left - high.astype(jnp.float32)).astype(jnp.bfloat16)
    dims = (((0,), (0,)), ((), ()))
    return lax.dot_general(
        high, right, dims, preferred_element_type=jnp.float32
    ) + lax.dot_general(low, right, dims, preferred_element_type=jnp.float32)


def expert_rows(mixing, summed, expert):
    total = mixing[0, expert] * summed[:, 0]
    for k in range(1, summed.shape[1]):
        total = total + mixing[k, expert] * summed[:, k]
    return total


def adam_rows(gradient, clip, params, moment_one, moment_two):
    clipped = clip * gradient
    new_one = beta_one * moment_one + (1.0 - beta_one) * clipped
    new_two = beta_two * moment_two + (1.0 - beta_two) * clipped * clipped
    first_fix = 1.0 - beta_one**STEP
    second_fix = 1.0 - beta_two**STEP
    direction = new_one / first_fix / (jnp.sqrt(new_two / second_fix) + adam_eps)
    return params - learn_rate * (direction + decay_rate * params), new_one, new_two


def exchange_kernel(
    shards, reps, norm_limit, mixing, pieces, params, moment_one, moment_two,
    summed, clip_out, weights, pair_in, pair_sum, slices, norms,
    pair_sem, slice_send, slice_recv, rep_send, rep_recv, norm_send, norm_recv,
    z_send, z_recv, y_send, y_recv, x_send, x_recv, core_send, core_recv,
):
    shard, rep = lax.axis_index("shard"), lax.axis_index("rep")
    planes, columns, depth = reps // 2, 2, shards // 2
    x, core = rep // 2, rep % 2
    z, y = shard // 2, shard % 2
    devices = shards * reps
    me = shard * reps + rep
    experts = params.shape[0]
    tags = summed.shape[1]

    barrier = pltpu.get_barrier_semaphore()
    for j in range(1, devices):
        other = lax.rem(me + j, devices)
        pl.semaphore_signal(
            barrier, inc=1, device_id=(other // reps, lax.rem(other, reps)), device_id_type=MESH
        )
    pl.semaphore_wait(barrier, devices - 1)

    def send(src, dst, send_sem, recv_sem, to):
        copy = pltpu.make_async_remote_copy(
            src_ref=src, dst_ref=dst, send_sem=send_sem, recv_sem=recv_sem,
            device_id=to, device_id_type=MESH,
        )
        copy.start()
        return copy

    sibling = (shard, x * 2 + 1 - core)
    started = []

    pair = [
        send(pieces.at[1 - core, i], pair_in.at[i], pair_sem.at[0, i], pair_sem.at[1, i], sibling)
        for i in range(planes)
    ]
    for i in range(planes):
        pair[i].wait_recv()
        pair_sum[i] = (
            pieces[core, i].astype(jnp.float32) + pair_in[i].astype(jnp.float32)
        ).astype(jnp.bfloat16)
    started += pair

    arriving = []
    for ds in range(shards):
        for dx in range(planes):
            if ds == 0 and dx == 0:
                continue
            to_x, to_s = lax.rem(x + dx, planes), lax.rem(shard + ds, shards)
            j = dx * shards + ds
            arriving.append(
                send(
                    pair_sum.at[to_x, to_s], slices.at[j], slice_send.at[j], slice_recv.at[j],
                    (to_s, to_x * 2 + core),
                )
            )
    total = pair_sum[x, shard].astype(jnp.float32)
    for copy in arriving:
        copy.wait_recv()
    for j in range(1, planes * shards):
        total = total + slices[j].astype(jnp.float32)
    started += arriving
    own = total.reshape(tags, 8, total.shape[-1])
    summed[rep] = own

    shared = []
    for j in range(1, reps):
        shared.append(
            send(
                summed.at[rep], summed.at[rep], rep_send.at[j], rep_recv.at[j],
                (shard, lax.rem(rep + j, reps)),
            )
        )
    squares = jnp.zeros(own.shape[1:], jnp.float32)
    for e in range(experts):
        gradient = expert_rows(mixing, own[None], e)[0]
        squares = squares + gradient * gradient
    norms[me] = squares
    normed = []
    for j in range(1, devices):
        other = lax.rem(me + j, devices)
        normed.append(
            send(
                norms.at[me], norms.at[me], norm_send.at[j], norm_recv.at[j],
                (other // reps, lax.rem(other, reps)),
            )
        )
    for copy in shared:
        copy.wait_recv()
    for copy in normed:
        copy.wait_recv()
    started += shared + normed
    square_sum = jnp.sum(jnp.sum(norms[...], axis=0), axis=(0, 1), keepdims=True)
    clip = jnp.minimum(1.0, norm_limit / (jnp.sqrt(square_sum) + 1e-06))
    clip_out[...] = jnp.broadcast_to(clip, clip_out.shape)

    half = experts // 2
    span = (half * 5) // 8
    only = half - span
    first = core * half + x * only
    cross = core * half + x * (half - only)
    cross_other = core * half + (1 - x) * (half - only)
    rows = weights.shape[1] // shards

    def update(i, carry):
        e = lax.rem(first + i, experts)
        new_params, _, _ = adam_rows(
            expert_rows(mixing, summed, e), clip, params[e], moment_one[e], moment_two[e]
        )
        weights[e, pl.ds(pl.multiple_of(shard * rows, rows), rows), :] = new_params.reshape(
            rows, new_params.shape[-1]
        ).astype(jnp.bfloat16)
        return carry

    lax.fori_loop(0, span, update, 0)

    def pass_on(begin, count, owner, send_sem, recv_sem, to):
        block = weights.at[
            pl.ds(begin, count), pl.ds(pl.multiple_of(owner * rows, rows), rows), :
        ]
        copy = send(block, block, send_sem, recv_sem, to)
        started.append(copy)
        return copy

    beside = (z * 2 + 1 - y, rep)
    across = (shard, (1 - x) * 2 + core)
    along, turned = [None] * depth, [None] * depth
    turned[0] = pass_on(first, span, shard, y_send.at[0], y_recv.at[0], beside)
    for d in range(1, depth):
        to = lax.rem(z + d, depth) * 2 + y
        along[d] = pass_on(first, span, shard, z_send.at[d], z_recv.at[d], (to, rep))
    lax.fori_loop(span, experts, update, 0)

    crossed, paired = [], []

    def arrived(slot, owner):
        crossed.append(
            (slot, owner, pass_on(cross, only, owner, x_send.at[slot], x_recv.at[slot], across))
        )
        paired.append(
            pass_on(first, span, owner, core_send.at[slot], core_recv.at[slot], sibling)
        )

    for d in range(depth):
        if d > 0:
            along[d].wait_recv()
            owner = lax.rem(z + depth - d, depth) * 2 + y
            turned[d] = pass_on(first, span, owner, y_send.at[d], y_recv.at[d], beside)
            arrived(d, owner)
        turned[d].wait_recv()
        arrived(depth + d, lax.rem(z + depth - d, depth) * 2 + 1 - y)
    for slot, owner, copy in crossed:
        copy.wait_recv()
        at = shards + slot
        paired.append(
            pass_on(cross_other, only, owner, core_send.at[at], core_recv.at[at], sibling)
        )
    for copy in paired:
        copy.wait_recv()
    for copy in started:
        copy.wait_send()


def finish_kernel(
    mixing, summed, clip, params, moment_one, moment_two, gathered,
    new_params, new_one, new_two, weights, sem,
):
    step = pl.program_id(0)
    copy = pltpu.make_async_copy(gathered, weights, sem)

    @pl.when(step == 0)
    def _():
        copy.start()

    block = params.shape[0]
    factor = clip[0:1, 0:1]

    def update(i, carry):
        gradient = expert_rows(mixing, summed, step * block + i)
        new_params[i], new_one[i], new_two[i] = adam_rows(
            gradient, factor, params[i], moment_one[i], moment_two[i]
        )
        return carry

    lax.fori_loop(0, block, update, 0, unroll=2)

    @pl.when(step == pl.num_programs(0) - 1)
    def _():
        copy.wait()


def kernel_local(shards, reps, *args):
    (
        node_feat, node_cot, edge_length, atom_count, edge_count, edge_source, edge_target,
        dataset_tag, charge_tag, spin_tag, dataset_gain, charge_gain, spin_gain,
        params, moment_one, moment_two,
    ) = args
    experts, own_channels, parts, channels = params.shape
    mixing = mixing_table(dataset_gain, charge_gain, spin_gain)
    tags = mixing.shape[0]
    planes = reps // 2
    f32, bf16 = jnp.float32, jnp.bfloat16
    vmem = pl.BlockSpec(memory_space=pltpu.VMEM)
    smem = pl.BlockSpec(memory_space=pltpu.SMEM)
    dma = pltpu.SemaphoreType.DMA
    slice_rows = tags * 8

    pieces = pl.pallas_call(
        functools.partial(partial_kernel, charge_gain.shape[0], spin_gain.shape[0], reps),
        out_shape=jax.ShapeDtypeStruct((2, planes, shards, slice_rows, channels), bf16),
        in_specs=[vmem, vmem, vmem, smem, smem, vmem, vmem, smem, smem, smem],
        out_specs=vmem,
        scratch_shapes=[pltpu.VMEM((tags, channels * parts, channels), f32)],
        compiler_params=pltpu.CompilerParams(vmem_limit_bytes=24 * MIB),
        name="partial_sums",
    )(
        node_feat, node_cot, edge_length, atom_count, edge_count, edge_source, edge_target,
        dataset_tag, charge_tag, spin_tag,
    )
    rows = own_channels * parts
    states = [a.reshape(experts, reps, 8, channels) for a in (params, moment_one, moment_two)]
    norm_limit = math.sqrt(experts * parts * channels * channels)
    depth = shards // 2
    summed, clip, gathered = pl.pallas_call(
        functools.partial(exchange_kernel, shards, reps, norm_limit),
        out_shape=(
            jax.ShapeDtypeStruct((reps, tags, 8, channels), f32),
            jax.ShapeDtypeStruct((8, channels), f32),
            jax.ShapeDtypeStruct((experts, shards * rows, channels), bf16),
        ),
        in_specs=[smem, vmem, vmem, vmem, vmem],
        out_specs=(vmem, vmem, vmem),
        scratch_shapes=[
            pltpu.VMEM((planes, shards, slice_rows, channels), bf16),
            pltpu.VMEM((planes, shards, slice_rows, channels), bf16),
            pltpu.VMEM((planes * shards, slice_rows, channels), bf16),
            pltpu.VMEM((shards * reps, 8, channels), f32),
            dma((2, planes)),
            dma((planes * shards,)),
            dma((planes * shards,)),
            dma((reps,)),
            dma((reps,)),
            dma((shards * reps,)),
            dma((shards * reps,)),
            dma((depth,)),
            dma((depth,)),
            dma((depth,)),
            dma((depth,)),
            dma((shards,)),
            dma((shards,)),
            dma((2 * shards,)),
            dma((2 * shards,)),
        ],
        compiler_params=pltpu.CompilerParams(
            collective_id=0, has_side_effects=True, vmem_limit_bytes=24 * MIB
        ),
        name="exchange",
    )(mixing, pieces, *states)

    steps = 4
    block = pl.BlockSpec((experts // steps, reps, 8, channels), lambda i: (i, 0, 0, 0))
    state = jax.ShapeDtypeStruct(states[0].shape, f32)
    anywhere = pl.BlockSpec(memory_space=pl.ANY)
    outs = pl.pallas_call(
        finish_kernel,
        grid=(steps,),
        out_shape=(state, state, state, jax.ShapeDtypeStruct(gathered.shape, bf16)),
        in_specs=[smem, vmem, vmem, block, block, block, anywhere],
        out_specs=(block, block, block, anywhere),
        scratch_shapes=[dma],
        compiler_params=pltpu.CompilerParams(vmem_limit_bytes=16 * MIB),
        name="finish",
    )(mixing, summed, clip, *states, gathered)
    local_states = [a.reshape(params.shape) for a in outs[:3]]
    return (*local_states, outs[3].reshape(experts, shards * own_channels, parts, channels))


def solution(mesh):
    placed = (
        P(("shard", "rep"), None, None),
        P(("shard", "rep"), None, None),
        P(("shard", "rep"), None),
        P(("shard", "rep")),
        P(("shard", "rep")),
        P(("shard", "rep"), None),
        P(("shard", "rep"), None),
        P(("shard", "rep")),
        P(("shard", "rep")),
        P(("shard", "rep")),
        P(),
        P(),
        P(),
        P(None, "shard", None, None),
        P(None, "shard", None, None),
        P(None, "shard", None, None),
    )
    shards, reps = mesh.shape["shard"], mesh.shape["rep"]

    def local(*args):
        params = args[13]
        if reps == 4 and shards % 2 == 0 and params.shape[1] * params.shape[2] == 8 * reps:
            return kernel_local(shards, reps, *args)
        return plain_local(*args)

    return jax.shard_map(
        local,
        mesh=mesh,
        in_specs=placed,
        out_specs=(
            P(None, "shard", None, None),
            P(None, "shard", None, None),
            P(None, "shard", None, None),
            P(),
        ),
        check_vma=False,
    )
```

```python
import functools
import math

import jax
import jax.numpy as jnp
from jax import lax
from jax.experimental import pallas as pl
from jax.experimental.pallas import tpu as pltpu
from jax.sharding import PartitionSpec as P

STEP = 10


beta_one = 0.9
beta_two = 0.999
adam_eps = 1e-08
learn_rate = 0.01
decay_rate = 0.01
cutoff_radius = 6.0


def envelope(length):
    ratio = length / cutoff_radius
    return 1.0 - 21.0 * ratio**5 + 35.0 * ratio**6 - 15.0 * ratio**7


def mixing_table(dataset_gain, charge_gain, spin_gain):
    product_table = (
        dataset_gain[:, None, None, :] * charge_gain[None, :, None, :] * spin_gain[None, None, :, :]
    )
    product_table = product_table.reshape(-1, product_table.shape[-1])
    return product_table / jnp.sum(product_table, axis=1, keepdims=True)


def onehot_rows(dataset_tag, charge_tag, spin_tag, charge_count, spin_count, row_total):
    tag_rows = (dataset_tag * charge_count + charge_tag) * spin_count + spin_tag
    return (tag_rows[:, None] == jnp.arange(row_total, dtype=jnp.int32)[None, :]).astype(
        jnp.float32
    )


def select_rows(node_rows, slot_ids):
    atom_ids = lax.broadcasted_iota(jnp.int32, (1, node_rows.shape[0]), 1)
    selector = (slot_ids[:, None] == atom_ids).astype(jnp.bfloat16)
    return jnp.dot(selector, node_rows, preferred_element_type=jnp.float32)


def system_product(items):
    feat_rows, cot_rows, length_row, atoms_here, edges_here, source_row, target_row = items
    atom_slots = feat_rows.shape[0]
    edge_input = (select_rows(feat_rows, source_row) * envelope(length_row)[:, None]).astype(
        jnp.bfloat16
    )
    slot_index = lax.broadcasted_iota(jnp.int32, source_row.shape, 0)
    live_mask = (slot_index < edges_here).astype(jnp.float32)
    factor = live_mask * (float(atom_slots) / atoms_here.astype(jnp.float32))
    edge_grad = (select_rows(cot_rows, target_row) * factor[:, None]).astype(jnp.bfloat16)
    return lax.dot_general(
        edge_input, edge_grad, (((0,), (0,)), ((), ())), preferred_element_type=jnp.float32
    )


def adam_update(gradients, params, moment_one, moment_two, square_sum, norm_limit):
    clip_factor = jnp.minimum(1.0, norm_limit / (jnp.sqrt(square_sum) + 1e-06))
    clipped = clip_factor * gradients
    new_one = beta_one * moment_one + (1.0 - beta_one) * clipped
    new_two = beta_two * moment_two + (1.0 - beta_two) * clipped * clipped
    first_fix = 1.0 - beta_one**STEP
    second_fix = 1.0 - beta_two**STEP
    direction = new_one / first_fix / (jnp.sqrt(new_two / second_fix) + adam_eps)
    new_params = params - learn_rate * (direction + decay_rate * params)
    return (new_params, new_one, new_two)


def plain_local(
    node_feat,
    node_cot,
    edge_length,
    atom_count,
    edge_count,
    edge_source,
    edge_target,
    dataset_tag,
    charge_tag,
    spin_tag,
    dataset_gain,
    charge_gain,
    spin_gain,
    params,
    moment_one,
    moment_two,
):
    channels = node_feat.shape[2] // 2
    mixing = mixing_table(dataset_gain, charge_gain, spin_gain)
    tag_onehot = onehot_rows(
        dataset_tag, charge_tag, spin_tag, charge_gain.shape[0], spin_gain.shape[0], mixing.shape[0]
    )
    products = lax.map(
        system_product,
        (node_feat, node_cot, edge_length, atom_count, edge_count, edge_source, edge_target),
    )
    real_part = products[:, :channels, :channels] + products[:, channels:, channels:]
    imag_part = products[:, :channels, channels:] - products[:, channels:, :channels]
    system_grad = jnp.stack([real_part, imag_part], axis=2)
    local_term = jnp.einsum(
        "sk,scto->ckto", tag_onehot, system_grad, precision=lax.Precision.HIGHEST
    )
    summed = lax.psum_scatter(local_term, "shard", scatter_dimension=0, tiled=True)
    summed = lax.psum(summed, "rep")
    gradients = jnp.einsum("ke,ckto->ecto", mixing, summed, precision=lax.Precision.HIGHEST)
    square_sum = lax.psum(jnp.sum(gradients * gradients), "shard")
    norm_limit = math.sqrt(mixing.shape[1] * 2 * channels * channels)
    new_params, new_one, new_two = adam_update(
        gradients, params, moment_one, moment_two, square_sum, norm_limit
    )
    full_weights = lax.all_gather(new_params.astype(jnp.bfloat16), "shard", axis=1, tiled=True)
    return (new_params, new_one, new_two, full_weights)


MIB = 1024 * 1024
MESH = pl.DeviceIdType.MESH


def split_dot(left, right, contract):
    high = right.astype(jnp.bfloat16)
    low = (right - high.astype(jnp.float32)).astype(jnp.bfloat16)
    dims = (contract, ((), ()))
    return lax.dot_general(
        left, high, dims, preferred_element_type=jnp.float32
    ) + lax.dot_general(left, low, dims, preferred_element_type=jnp.float32)


def split_dot_left(left, right):
    high = left.astype(jnp.bfloat16)
    low = (left - high.astype(jnp.float32)).astype(jnp.bfloat16)
    dims = (((0,), (0,)), ((), ()))
    return lax.dot_general(
        high, right, dims, preferred_element_type=jnp.float32
    ) + lax.dot_general(low, right, dims, preferred_element_type=jnp.float32)


def expert_rows(mixing, summed, expert):
    total = mixing[0, expert] * summed[:, 0]
    for k in range(1, summed.shape[1]):
        total = total + mixing[k, expert] * summed[:, k]
    return total


def adam_rows(gradient, clip, params, moment_one, moment_two):
    clipped = clip * gradient
    new_one = beta_one * moment_one + (1.0 - beta_one) * clipped
    new_two = beta_two * moment_two + (1.0 - beta_two) * clipped * clipped
    first_fix = 1.0 - beta_one**STEP
    second_fix = 1.0 - beta_two**STEP
    direction = new_one / first_fix / (jnp.sqrt(new_two / second_fix) + adam_eps)
    return params - learn_rate * (direction + decay_rate * params), new_one, new_two


def system_sums(feat, cot, weight, source, target, atoms, edges, products):
    systems, slots, width = feat.shape
    channels = width // 2
    lanes = source.shape[1]

    def one_system(s, carry):
        slot_index = lax.broadcasted_iota(jnp.int32, (1, lanes), 1)
        atom_index = lax.broadcasted_iota(jnp.int32, (slots, lanes), 0)
        count = jnp.full((1, lanes), atoms[s], jnp.int32).astype(jnp.float32)
        factor = jnp.where(slot_index < edges[s], float(slots) / count, 0.0)
        row = weight[pl.ds(s, 1), :] * factor
        left = jnp.where(atom_index == source[pl.ds(s, 1), :], row, 0.0).astype(jnp.bfloat16)
        right = jnp.where(atom_index == target[pl.ds(s, 1), :], 1.0, 0.0).astype(jnp.bfloat16)
        pairs = lax.dot_general(
            right, left, (((1,), (1,)), ((), ())), preferred_element_type=jnp.float32
        )
        mixed = split_dot_left(pairs, cot[s])
        real, imag = mixed[:, :channels], mixed[:, channels:]
        block = jnp.concatenate(
            [
                jnp.concatenate([real, imag], axis=1),
                jnp.concatenate([imag, -real], axis=1),
            ],
            axis=0,
        )
        rows = feat[s]
        stacked = jnp.concatenate([rows[:, :channels], rows[:, channels:]], axis=0)
        product = split_dot(stacked, block, ((0,), (0,)))
        products[s, pl.ds(0, channels, stride=2), :] = product[:, :channels]
        products[s, pl.ds(1, channels, stride=2), :] = product[:, channels:]
        return carry

    lax.fori_loop(0, systems, one_system, 0, unroll=UNROLL_SYSTEMS)


UNROLL_SYSTEMS = 4


def whole_kernel(
    shards, reps, norm_limit,
    feat_in, cot_in, length_in, atoms_in, edges_in, source_in, target_in,
    dataset_in, charge_in, spin_in, dataset_gain_in, charge_gain_in, spin_gain_in,
    params_in, one_in, two_in,
    new_params_out, new_one_out, new_two_out, weights,
    feat, cot, length, source, target, dataset_gain, charge_gain, spin_gain,
    params, moment_one, moment_two, new_params, new_one, new_two, table, atoms, edges, dataset, charge, spin, mixing,
    products, pieces, pair_in, pair_sum, slices, summed, norms,
    fetch_sem, store_sem, table_sem, pair_sem, slice_send, slice_recv, rep_send, rep_recv,
    norm_send, norm_recv, z_send, z_recv, y_send, y_recv, x_send, x_recv, core_send, core_recv,
):
    shard, rep = lax.axis_index("shard"), lax.axis_index("rep")
    planes, depth = reps // 2, shards // 2
    x, core = rep // 2, rep % 2
    z, y = shard // 2, shard % 2
    devices = shards * reps
    me = shard * reps + rep
    experts = params.shape[0]
    tags = summed.shape[1]

    fetches = [
        pltpu.make_async_copy(src, dst, fetch_sem.at[i])
        for i, (src, dst) in enumerate(
            (
                (source_in, source), (target_in, target), (length_in, length),
                (atoms_in, atoms), (edges_in, edges), (cot_in, cot), (feat_in, feat),
                (dataset_in, dataset), (charge_in, charge), (spin_in, spin),
                (dataset_gain_in, dataset_gain), (charge_gain_in, charge_gain),
                (spin_gain_in, spin_gain),
                (params_in, params), (one_in, moment_one), (two_in, moment_two),
            )
        )
    ]
    for fetch in fetches:
        fetch.start()

    barrier = pltpu.get_barrier_semaphore()
    for j in range(1, devices):
        other = lax.rem(me + j, devices)
        pl.semaphore_signal(
            barrier, inc=1, device_id=(other // reps, lax.rem(other, reps)), device_id_type=MESH
        )

    for fetch in fetches[:13]:
        fetch.wait()
    charges, spins = charge_gain.shape[0], spin_gain.shape[0]
    table[...] = jnp.zeros_like(table)
    for k in range(tags):
        d, c, s = k // (charges * spins), (k // spins) % charges, k % spins
        line = dataset_gain[d : d + 1, :] * charge_gain[c : c + 1, :] * spin_gain[s : s + 1, :]
        table[k : k + 1, 0:experts] = line / jnp.sum(line, axis=1, keepdims=True)
    to_scalars = pltpu.make_async_copy(table, mixing, table_sem)
    to_scalars.start()

    length[...] = envelope(length[...])
    system_sums(feat, cot, length, source, target, atoms, edges, products)

    systems, _, channels = products.shape
    rows_of = [
        (dataset[s] * charges + charge[s]) * spins + spin[s] for s in range(systems)
    ]
    takes = [
        [jnp.where(rows_of[s] == k, 1.0, 0.0) for s in range(systems)] for k in range(tags)
    ]

    def group(i, carry):
        at = pl.multiple_of(i * 8, 8)
        terms = [products[s, pl.ds(at, 8), :] for s in range(systems)]
        sums = []
        for k in range(tags):
            total = takes[k][0] * terms[0]
            for s in range(1, systems):
                total = total + takes[k][s] * terms[s]
            sums.append(total)
        owner, r = i // reps, lax.rem(i, reps)
        pieces[lax.rem(r, 2), r // 2, owner] = jnp.concatenate(sums, axis=0)
        return carry

    lax.fori_loop(0, devices, group, 0, unroll=2)
    pl.semaphore_wait(barrier, devices - 1)

    def send(src, dst, send_sem, recv_sem, to):
        copy = pltpu.make_async_remote_copy(
            src_ref=src, dst_ref=dst, send_sem=send_sem, recv_sem=recv_sem,
            device_id=to, device_id_type=MESH,
        )
        copy.start()
        return copy

    sibling = (shard, x * 2 + 1 - core)
    started = []

    order = [(dx, lax.rem(x + dx, planes)) for dx in range(planes - 1, -1, -1)]
    pair = [
        send(
            pieces.at[1 - core, i], pair_in.at[i],
            pair_sem.at[0, dx], pair_sem.at[1, dx], sibling,
        )
        for dx, i in order
    ]
    started += pair
    arriving = []
    for at, (dx, i) in enumerate(order):
        pair[at].wait_recv()
        pair_sum[i] = pieces[core, i] + pair_in[i]
        for ds in range(shards):
            if ds == 0 and dx == 0:
                continue
            to_s = lax.rem(shard + ds, shards)
            j = dx * shards + ds
            arriving.append(
                send(
                    pair_sum.at[i, to_s], slices.at[j], slice_send.at[j], slice_recv.at[j],
                    (to_s, i * 2 + core),
                )
            )
    to_scalars.wait()
    total = pair_sum[x, shard]
    for copy in arriving:
        copy.wait_recv()
    for j in range(1, planes * shards):
        total = total + slices[j]
    started += arriving
    own = total.reshape(tags, 8, total.shape[-1])
    summed[rep] = own

    shared = []
    for j in range(1, reps):
        shared.append(
            send(
                summed.at[rep], summed.at[rep], rep_send.at[j], rep_recv.at[j],
                (shard, lax.rem(rep + j, reps)),
            )
        )
    squares = jnp.zeros(own.shape[1:], jnp.float32)
    for e in range(experts):
        gradient = expert_rows(mixing, own[None], e)[0]
        squares = squares + gradient * gradient
    norms[me] = squares
    normed = []
    for j in range(1, devices):
        other = lax.rem(me + j, devices)
        normed.append(
            send(
                norms.at[me], norms.at[me], norm_send.at[j], norm_recv.at[j],
                (other // reps, lax.rem(other, reps)),
            )
        )
    for fetch in fetches[13:]:
        fetch.wait()
    for copy in shared:
        copy.wait_recv()
    for copy in normed:
        copy.wait_recv()
    started += shared + normed
    square_sum = jnp.sum(jnp.sum(norms[...], axis=0), axis=(0, 1), keepdims=True)
    clip = jnp.minimum(1.0, norm_limit / (jnp.sqrt(square_sum) + 1e-06))

    half = experts // 2
    span = (half * 5) // 8
    cross = half - span
    first = core * half + x * cross
    chunks = (
        (core * half + x * span, cross, True),
        (core * half + cross, span - cross, False),
    )
    cross_other = core * half + (1 - x) * span
    rows = weights.shape[1] // shards

    def update(begin):
        def one(i, carry):
            e = lax.rem(begin + i, experts)
            new_params[e], new_one[e], new_two[e] = adam_rows(
                expert_rows(mixing, summed, e), clip, params[e], moment_one[e], moment_two[e]
            )
            weights[e, pl.ds(pl.multiple_of(shard * rows, rows), rows), :] = (
                new_params[e].reshape(rows, weights.shape[-1]).astype(jnp.bfloat16)
            )
            return carry

        return one

    def pass_on(begin, count, owner, send_sem, recv_sem, to):
        block = weights.at[
            pl.ds(begin, count), pl.ds(pl.multiple_of(owner * rows, rows), rows), :
        ]
        copy = send(block, block, send_sem, recv_sem, to)
        started.append(copy)
        return copy

    beside = (z * 2 + 1 - y, rep)
    across = (shard, (1 - x) * 2 + core)
    along = [[None] * depth for _ in chunks]
    turned = [[None] * depth for _ in chunks]
    for n, (begin, count, _) in enumerate(chunks):
        lax.fori_loop(0, count, update(begin), 0, unroll=count)
        for d in range(1, depth):
            to = lax.rem(z + d, depth) * 2 + y
            along[n][d] = pass_on(
                begin, count, shard, z_send.at[n, d], z_recv.at[n, d], (to, rep)
            )
        turned[n][0] = pass_on(begin, count, shard, y_send.at[n, 0], y_recv.at[n, 0], beside)
    lax.fori_loop(0, experts - span, update(first + span), 0, unroll=2)
    stores = [
        pltpu.make_async_copy(src, dst, store_sem.at[i])
        for i, (src, dst) in enumerate(
            ((new_params, new_params_out), (new_one, new_one_out), (new_two, new_two_out))
        )
    ]
    for store in stores:
        store.start()

    crossed, paired = [], []

    def arrived(n, slot, owner):
        begin, count, crosses = chunks[n]
        if crosses:
            copy = pass_on(begin, count, owner, x_send.at[slot], x_recv.at[slot], across)
            crossed.append((slot, owner, copy))
        paired.append(
            pass_on(begin, count, owner, core_send.at[n, slot], core_recv.at[n, slot], sibling)
        )

    def from_across():
        slot, owner, copy = crossed.pop(0)
        copy.wait_recv()
        paired.append(
            pass_on(
                cross_other, cross, owner,
                core_send.at[len(chunks), slot], core_recv.at[len(chunks), slot], sibling,
            )
        )

    for n, (begin, count, _) in enumerate(chunks):
        turned[n][0].wait_recv()
        arrived(n, depth, z * 2 + 1 - y)
        for d in range(1, depth):
            along[n][d].wait_recv()
            owner = lax.rem(z + depth - d, depth) * 2 + y
            turned[n][d] = pass_on(
                begin, count, owner, y_send.at[n, d], y_recv.at[n, d], beside
            )
            arrived(n, d, owner)
        if n == 0:
            continue
        for d in range(1, depth):
            turned[n - 1][d].wait_recv()
            arrived(n - 1, depth + d, lax.rem(z + depth - d, depth) * 2 + 1 - y)
    for _ in range(depth):
        from_across()
    for d in range(1, depth):
        turned[-1][d].wait_recv()
        arrived(len(chunks) - 1, depth + d, lax.rem(z + depth - d, depth) * 2 + 1 - y)
    while crossed:
        from_across()
    for copy in paired:
        copy.wait_recv()
    for copy in started:
        copy.wait_send()
    for store in stores:
        store.wait()


def finish_kernel(*refs):
    count = (len(refs) - 1) // 2
    sem = refs[-1]
    copies = [
        pltpu.make_async_copy(refs[i], refs[count + i], sem.at[i]) for i in range(count)
    ]
    for copy in copies:
        copy.start()
    for copy in copies:
        copy.wait()


def kernel_local(shards, reps, *args):
    params = args[13]
    experts, own_channels, parts, channels = params.shape
    planes, depth, devices = reps // 2, shards // 2, shards * reps
    f32, bf16, i32 = jnp.float32, jnp.bfloat16, jnp.int32
    dma = pltpu.SemaphoreType.DMA
    anywhere = pl.BlockSpec(memory_space=pl.ANY)
    vmem = pl.BlockSpec(memory_space=pltpu.VMEM)
    systems, lanes = args[2].shape
    gains = args[10:13]
    tags = gains[0].shape[0] * gains[1].shape[0] * gains[2].shape[0]
    slice_rows = tags * 8
    rows = own_channels * parts
    states = [a.reshape(experts, reps, 8, channels) for a in args[13:16]]
    state = (experts, reps, 8, channels)
    norm_limit = math.sqrt(experts * parts * channels * channels)
    chunk_total = 2

    def held(array):
        return pltpu.VMEM(array.shape, array.dtype)

    def pairs(*shape):
        return [dma(shape), dma(shape)]

    outs = [jax.ShapeDtypeStruct(state, f32)] * 3
    outs.append(jax.ShapeDtypeStruct((experts, shards * rows, channels), bf16))
    results = pl.pallas_call(
        functools.partial(whole_kernel, shards, reps, norm_limit),
        out_shape=outs,
        in_specs=[anywhere] * 16,
        out_specs=[anywhere] * 3 + [vmem],
        scratch_shapes=[
            held(args[0]), held(args[1]), held(args[2]), held(args[5]), held(args[6]),
            *[held(a) for a in gains],
            *[pltpu.VMEM(state, f32)] * 6,
            pltpu.VMEM((tags, 128), f32),
            *[pltpu.SMEM((systems,), i32)] * 5,
            pltpu.SMEM((tags, 128), f32),
            pltpu.VMEM((systems, channels * parts, channels), f32),
            pltpu.VMEM((2, planes, shards, slice_rows, channels), f32),
            pltpu.VMEM((planes, shards, slice_rows, channels), f32),
            pltpu.VMEM((planes, shards, slice_rows, channels), f32),
            pltpu.VMEM((planes * shards, slice_rows, channels), f32),
            pltpu.VMEM((reps, tags, 8, channels), f32),
            pltpu.VMEM((devices, 8, channels), f32),
            dma((16,)),
            dma((3,)),
            dma,
            dma((2, planes)),
            *pairs(planes * shards),
            *pairs(reps),
            *pairs(devices),
            *pairs(chunk_total, depth),
            *pairs(chunk_total, depth),
            *pairs(shards),
            *pairs(chunk_total + 1, shards),
        ],
        compiler_params=pltpu.CompilerParams(
            collective_id=0, has_side_effects=True, vmem_limit_bytes=60 * MIB
        ),
        name="whole",
    )(*args[:13], *states)

    outs = pl.pallas_call(
        finish_kernel,
        out_shape=outs,
        in_specs=[anywhere] * 4,
        out_specs=[anywhere] * 4,
        scratch_shapes=[dma((4,))],
        compiler_params=pltpu.CompilerParams(vmem_limit_bytes=60 * MIB),
        name="finish",
    )(*results)
    local_states = [a.reshape(params.shape) for a in outs[:3]]
    return (*local_states, outs[3].reshape(experts, shards * own_channels, parts, channels))


def solution(mesh):
    placed = (
        P(("shard", "rep"), None, None),
        P(("shard", "rep"), None, None),
        P(("shard", "rep"), None),
        P(("shard", "rep")),
        P(("shard", "rep")),
        P(("shard", "rep"), None),
        P(("shard", "rep"), None),
        P(("shard", "rep")),
        P(("shard", "rep")),
        P(("shard", "rep")),
        P(),
        P(),
        P(),
        P(None, "shard", None, None),
        P(None, "shard", None, None),
        P(None, "shard", None, None),
    )
    shards, reps = mesh.shape["shard"], mesh.shape["rep"]

    def local(*args):
        params = args[13]
        if reps == 4 and shards % 2 == 0 and params.shape[1] * params.shape[2] == 8 * reps:
            return kernel_local(shards, reps, *args)
        return plain_local(*args)

    return jax.shard_map(
        local,
        mesh=mesh,
        in_specs=placed,
        out_specs=(
            P(None, "shard", None, None),
            P(None, "shard", None, None),
            P(None, "shard", None, None),
            P(),
        ),
        check_vma=False,
    )
```

```python
import functools
import math

import jax
import jax.numpy as jnp
from jax import lax
from jax.experimental import pallas as pl
from jax.experimental.pallas import tpu as pltpu
from jax.sharding import PartitionSpec as P

STEP = 10


beta_one = 0.9
beta_two = 0.999
adam_eps = 1e-08
learn_rate = 0.01
decay_rate = 0.01
cutoff_radius = 6.0


def envelope(length):
    ratio = length / cutoff_radius
    return 1.0 - 21.0 * ratio**5 + 35.0 * ratio**6 - 15.0 * ratio**7


def mixing_table(dataset_gain, charge_gain, spin_gain):
    product_table = (
        dataset_gain[:, None, None, :] * charge_gain[None, :, None, :] * spin_gain[None, None, :, :]
    )
    product_table = product_table.reshape(-1, product_table.shape[-1])
    return product_table / jnp.sum(product_table, axis=1, keepdims=True)


def onehot_rows(dataset_tag, charge_tag, spin_tag, charge_count, spin_count, row_total):
    tag_rows = (dataset_tag * charge_count + charge_tag) * spin_count + spin_tag
    return (tag_rows[:, None] == jnp.arange(row_total, dtype=jnp.int32)[None, :]).astype(
        jnp.float32
    )


def select_rows(node_rows, slot_ids):
    atom_ids = lax.broadcasted_iota(jnp.int32, (1, node_rows.shape[0]), 1)
    selector = (slot_ids[:, None] == atom_ids).astype(jnp.bfloat16)
    return jnp.dot(selector, node_rows, preferred_element_type=jnp.float32)


def system_product(items):
    feat_rows, cot_rows, length_row, atoms_here, edges_here, source_row, target_row = items
    atom_slots = feat_rows.shape[0]
    edge_input = (select_rows(feat_rows, source_row) * envelope(length_row)[:, None]).astype(
        jnp.bfloat16
    )
    slot_index = lax.broadcasted_iota(jnp.int32, source_row.shape, 0)
    live_mask = (slot_index < edges_here).astype(jnp.float32)
    factor = live_mask * (float(atom_slots) / atoms_here.astype(jnp.float32))
    edge_grad = (select_rows(cot_rows, target_row) * factor[:, None]).astype(jnp.bfloat16)
    return lax.dot_general(
        edge_input, edge_grad, (((0,), (0,)), ((), ())), preferred_element_type=jnp.float32
    )


def adam_update(gradients, params, moment_one, moment_two, square_sum, norm_limit):
    clip_factor = jnp.minimum(1.0, norm_limit / (jnp.sqrt(square_sum) + 1e-06))
    clipped = clip_factor * gradients
    new_one = beta_one * moment_one + (1.0 - beta_one) * clipped
    new_two = beta_two * moment_two + (1.0 - beta_two) * clipped * clipped
    first_fix = 1.0 - beta_one**STEP
    second_fix = 1.0 - beta_two**STEP
    direction = new_one / first_fix / (jnp.sqrt(new_two / second_fix) + adam_eps)
    new_params = params - learn_rate * (direction + decay_rate * params)
    return (new_params, new_one, new_two)


def plain_local(
    node_feat,
    node_cot,
    edge_length,
    atom_count,
    edge_count,
    edge_source,
    edge_target,
    dataset_tag,
    charge_tag,
    spin_tag,
    dataset_gain,
    charge_gain,
    spin_gain,
    params,
    moment_one,
    moment_two,
):
    channels = node_feat.shape[2] // 2
    mixing = mixing_table(dataset_gain, charge_gain, spin_gain)
    tag_onehot = onehot_rows(
        dataset_tag, charge_tag, spin_tag, charge_gain.shape[0], spin_gain.shape[0], mixing.shape[0]
    )
    products = lax.map(
        system_product,
        (node_feat, node_cot, edge_length, atom_count, edge_count, edge_source, edge_target),
    )
    real_part = products[:, :channels, :channels] + products[:, channels:, channels:]
    imag_part = products[:, :channels, channels:] - products[:, channels:, :channels]
    system_grad = jnp.stack([real_part, imag_part], axis=2)
    local_term = jnp.einsum(
        "sk,scto->ckto", tag_onehot, system_grad, precision=lax.Precision.HIGHEST
    )
    summed = lax.psum_scatter(local_term, "shard", scatter_dimension=0, tiled=True)
    summed = lax.psum(summed, "rep")
    gradients = jnp.einsum("ke,ckto->ecto", mixing, summed, precision=lax.Precision.HIGHEST)
    square_sum = lax.psum(jnp.sum(gradients * gradients), "shard")
    norm_limit = math.sqrt(mixing.shape[1] * 2 * channels * channels)
    new_params, new_one, new_two = adam_update(
        gradients, params, moment_one, moment_two, square_sum, norm_limit
    )
    full_weights = lax.all_gather(new_params.astype(jnp.bfloat16), "shard", axis=1, tiled=True)
    return (new_params, new_one, new_two, full_weights)


MIB = 1024 * 1024
MESH = pl.DeviceIdType.MESH


def split_dot(left, right, contract):
    high = right.astype(jnp.bfloat16)
    low = (right - high.astype(jnp.float32)).astype(jnp.bfloat16)
    dims = (contract, ((), ()))
    return lax.dot_general(
        left, high, dims, preferred_element_type=jnp.float32
    ) + lax.dot_general(left, low, dims, preferred_element_type=jnp.float32)


def split_dot_left(left, right):
    high = left.astype(jnp.bfloat16)
    low = (left - high.astype(jnp.float32)).astype(jnp.bfloat16)
    dims = (((0,), (0,)), ((), ()))
    return lax.dot_general(
        high, right, dims, preferred_element_type=jnp.float32
    ) + lax.dot_general(low, right, dims, preferred_element_type=jnp.float32)


def expert_rows(mixing, summed, expert):
    total = mixing[0, expert] * summed[:, 0]
    for k in range(1, summed.shape[1]):
        total = total + mixing[k, expert] * summed[:, k]
    return total


def adam_rows(gradient, clip, params, moment_one, moment_two):
    clipped = clip * gradient
    new_one = beta_one * moment_one + (1.0 - beta_one) * clipped
    new_two = beta_two * moment_two + (1.0 - beta_two) * clipped * clipped
    first_fix = 1.0 - beta_one**STEP
    second_fix = 1.0 - beta_two**STEP
    direction = new_one / first_fix / (jnp.sqrt(new_two / second_fix) + adam_eps)
    return params - learn_rate * (direction + decay_rate * params), new_one, new_two


def system_sums(feat, cot, weight, source, target, atoms, edges, products):
    systems, slots, width = feat.shape
    channels = width // 2
    lanes = source.shape[1]

    def one_system(s, carry):
        slot_index = lax.broadcasted_iota(jnp.int32, (1, lanes), 1)
        atom_index = lax.broadcasted_iota(jnp.int32, (slots, lanes), 0)
        count = jnp.full((1, lanes), atoms[s], jnp.int32).astype(jnp.float32)
        factor = jnp.where(slot_index < edges[s], float(slots) / count, 0.0)
        row = weight[pl.ds(s, 1), :] * factor
        left = jnp.where(atom_index == source[pl.ds(s, 1), :], row, 0.0).astype(jnp.bfloat16)
        right = jnp.where(atom_index == target[pl.ds(s, 1), :], 1.0, 0.0).astype(jnp.bfloat16)
        pairs = lax.dot_general(
            right, left, (((1,), (1,)), ((), ())), preferred_element_type=jnp.float32
        )
        mixed = split_dot_left(pairs, cot[s])
        real, imag = mixed[:, :channels], mixed[:, channels:]
        block = jnp.concatenate(
            [
                jnp.concatenate([real, imag], axis=1),
                jnp.concatenate([imag, -real], axis=1),
            ],
            axis=0,
        )
        rows = feat[s]
        stacked = jnp.concatenate([rows[:, :channels], rows[:, channels:]], axis=0)
        product = split_dot(stacked, block, ((0,), (0,)))
        products[s, pl.ds(0, channels, stride=2), :] = product[:, :channels]
        products[s, pl.ds(1, channels, stride=2), :] = product[:, channels:]
        return carry

    lax.fori_loop(0, systems, one_system, 0, unroll=UNROLL_SYSTEMS)


UNROLL_SYSTEMS = 4


def whole_kernel(
    shards, reps, norm_limit,
    feat_in, cot_in, length_in, atoms_in, edges_in, source_in, target_in,
    dataset_in, charge_in, spin_in, dataset_gain_in, charge_gain_in, spin_gain_in,
    params_in, one_in, two_in,
    new_params_out, new_one_out, new_two_out, weights,
    feat, cot, length, source, target, dataset_gain, charge_gain, spin_gain,
    params, moment_one, moment_two, new_params, new_one, new_two, table, atoms, edges, dataset, charge, spin, mixing,
    products, pieces, pair_in, pair_sum, slices, z_sum, z_in, summed, norms,
    fetch_sem, store_sem, table_sem, pair_sem, slice_send, slice_recv, ahead_send, ahead_recv, rep_send, rep_recv,
    norm_send, norm_recv, z_send, z_recv, y_send, y_recv, x_send, x_recv, core_send, core_recv,
):
    shard, rep = lax.axis_index("shard"), lax.axis_index("rep")
    planes, depth = reps // 2, shards // 2
    x, core = rep // 2, rep % 2
    z, y = shard // 2, shard % 2
    devices = shards * reps
    me = shard * reps + rep
    experts = params.shape[0]
    tags = summed.shape[1]

    fetches = [
        pltpu.make_async_copy(src, dst, fetch_sem.at[i])
        for i, (src, dst) in enumerate(
            (
                (source_in, source), (target_in, target), (length_in, length),
                (atoms_in, atoms), (edges_in, edges), (cot_in, cot), (feat_in, feat),
                (dataset_in, dataset), (charge_in, charge), (spin_in, spin),
                (dataset_gain_in, dataset_gain), (charge_gain_in, charge_gain),
                (spin_gain_in, spin_gain),
                (params_in, params), (one_in, moment_one), (two_in, moment_two),
            )
        )
    ]
    for fetch in fetches:
        fetch.start()

    barrier = pltpu.get_barrier_semaphore()
    for j in range(1, devices):
        other = lax.rem(me + j, devices)
        pl.semaphore_signal(
            barrier, inc=1, device_id=(other // reps, lax.rem(other, reps)), device_id_type=MESH
        )

    for fetch in fetches[:13]:
        fetch.wait()
    charges, spins = charge_gain.shape[0], spin_gain.shape[0]
    table[...] = jnp.zeros_like(table)
    for k in range(tags):
        d, c, s = k // (charges * spins), (k // spins) % charges, k % spins
        line = dataset_gain[d : d + 1, :] * charge_gain[c : c + 1, :] * spin_gain[s : s + 1, :]
        table[k : k + 1, 0:experts] = line / jnp.sum(line, axis=1, keepdims=True)
    to_scalars = pltpu.make_async_copy(table, mixing, table_sem)
    to_scalars.start()

    length[...] = envelope(length[...])
    system_sums(feat, cot, length, source, target, atoms, edges, products)

    systems, _, channels = products.shape
    rows_of = [
        (dataset[s] * charges + charge[s]) * spins + spin[s] for s in range(systems)
    ]
    takes = [
        [jnp.where(rows_of[s] == k, 1.0, 0.0) for s in range(systems)] for k in range(tags)
    ]

    def group(i, carry):
        at = pl.multiple_of(i * 8, 8)
        terms = [products[s, pl.ds(at, 8), :] for s in range(systems)]
        sums = []
        for k in range(tags):
            total = takes[k][0] * terms[0]
            for s in range(1, systems):
                total = total + takes[k][s] * terms[s]
            sums.append(total)
        owner, r = i // reps, lax.rem(i, reps)
        pieces[lax.rem(r, 2), r // 2, owner] = jnp.concatenate(sums, axis=0)
        return carry

    lax.fori_loop(0, devices, group, 0, unroll=2)
    pl.semaphore_wait(barrier, devices - 1)

    def send(src, dst, send_sem, recv_sem, to):
        copy = pltpu.make_async_remote_copy(
            src_ref=src, dst_ref=dst, send_sem=send_sem, recv_sem=recv_sem,
            device_id=to, device_id_type=MESH,
        )
        copy.start()
        return copy

    sibling = (shard, x * 2 + 1 - core)
    started = []

    parts = [(dz, lax.rem(z + dz, depth)) for dz in [*range(1, depth), 0]]
    sides = [(dx, dy) for dx in range(planes) for dy in range(2) if (dx, dy) != (0, 0)]
    pair, sided, ahead = {}, {}, []
    for dz, to_z in parts:
        both = pl.ds(pl.multiple_of(to_z * 2, 2), 2)
        pair[dz] = send(
            pieces.at[1 - core, :, both], pair_in.at[:, both],
            pair_sem.at[0, dz], pair_sem.at[1, dz], sibling,
        )
    for dz, to_z in parts:
        both = pl.ds(pl.multiple_of(to_z * 2, 2), 2)
        pair[dz].wait_recv()
        pair_sum[:, both] = pieces[core, :, both] + pair_in[:, both]
        for n, (dx, dy) in enumerate(sides):
            to_x, to_y = lax.rem(x + dx, planes), lax.rem(y + dy, 2)
            sided[dz, n] = send(
                pair_sum.at[to_x, to_z * 2 + to_y], slices.at[dz, n],
                slice_send.at[dz, n], slice_recv.at[dz, n],
                (z * 2 + to_y, to_x * 2 + core),
            )
    for dz, to_z in parts:
        total = pair_sum[x, to_z * 2 + y]
        for n in range(len(sides)):
            sided[dz, n].wait_recv()
            total = total + slices[dz, n]
        if dz > 0:
            z_sum[dz] = total
            ahead.append(
                send(
                    z_sum.at[dz], z_in.at[dz], ahead_send.at[dz], ahead_recv.at[dz],
                    (to_z * 2 + y, rep),
                )
            )
    to_scalars.wait()
    for n, copy in enumerate(ahead):
        copy.wait_recv()
        total = total + z_in[n + 1]
    started += [*pair.values(), *sided.values(), *ahead]
    own = total.reshape(tags, 8, total.shape[-1])
    summed[rep] = own

    shared = []
    for j in range(1, reps):
        shared.append(
            send(
                summed.at[rep], summed.at[rep], rep_send.at[j], rep_recv.at[j],
                (shard, lax.rem(rep + j, reps)),
            )
        )
    squares = jnp.zeros(own.shape[1:], jnp.float32)
    for e in range(experts):
        gradient = expert_rows(mixing, own[None], e)[0]
        squares = squares + gradient * gradient
    norms[me] = squares
    normed = []
    for j in range(1, devices):
        other = lax.rem(me + j, devices)
        normed.append(
            send(
                norms.at[me], norms.at[me], norm_send.at[j], norm_recv.at[j],
                (other // reps, lax.rem(other, reps)),
            )
        )
    for fetch in fetches[13:]:
        fetch.wait()
    for copy in shared:
        copy.wait_recv()
    for copy in normed:
        copy.wait_recv()
    started += shared + normed
    square_sum = jnp.sum(jnp.sum(norms[...], axis=0), axis=(0, 1), keepdims=True)
    clip = jnp.minimum(1.0, norm_limit / (jnp.sqrt(square_sum) + 1e-06))

    half = experts // 2
    span = (half * 5) // 8
    cross = half - span
    first = core * half + x * cross
    chunks = (
        (core * half + x * span, cross, True),
        (core * half + cross, span - cross, False),
    )
    cross_other = core * half + (1 - x) * span
    rows = weights.shape[1] // shards

    def update(begin):
        def one(i, carry):
            e = lax.rem(begin + i, experts)
            new_params[e], new_one[e], new_two[e] = adam_rows(
                expert_rows(mixing, summed, e), clip, params[e], moment_one[e], moment_two[e]
            )
            weights[e, pl.ds(pl.multiple_of(shard * rows, rows), rows), :] = (
                new_params[e].reshape(rows, weights.shape[-1]).astype(jnp.bfloat16)
            )
            return carry

        return one

    def pass_on(begin, count, owner, send_sem, recv_sem, to):
        block = weights.at[
            pl.ds(begin, count), pl.ds(pl.multiple_of(owner * rows, rows), rows), :
        ]
        copy = send(block, block, send_sem, recv_sem, to)
        started.append(copy)
        return copy

    beside = (z * 2 + 1 - y, rep)
    across = (shard, (1 - x) * 2 + core)
    along = [[None] * depth for _ in chunks]
    turned = [[None] * depth for _ in chunks]
    for n, (begin, count, _) in enumerate(chunks):
        lax.fori_loop(0, count, update(begin), 0, unroll=count)
        for d in range(1, depth):
            to = lax.rem(z + d, depth) * 2 + y
            along[n][d] = pass_on(
                begin, count, shard, z_send.at[n, d], z_recv.at[n, d], (to, rep)
            )
        turned[n][0] = pass_on(begin, count, shard, y_send.at[n, 0], y_recv.at[n, 0], beside)
    lax.fori_loop(0, experts - span, update(first + span), 0, unroll=2)
    stores = [
        pltpu.make_async_copy(src, dst, store_sem.at[i])
        for i, (src, dst) in enumerate(
            ((new_params, new_params_out), (new_one, new_one_out), (new_two, new_two_out))
        )
    ]
    for store in stores:
        store.start()

    crossed, paired = [], []

    def arrived(n, slot, owner):
        begin, count, crosses = chunks[n]
        if crosses:
            copy = pass_on(begin, count, owner, x_send.at[slot], x_recv.at[slot], across)
            crossed.append((slot, owner, copy))
        paired.append(
            pass_on(begin, count, owner, core_send.at[n, slot], core_recv.at[n, slot], sibling)
        )

    def from_across():
        slot, owner, copy = crossed.pop(0)
        copy.wait_recv()
        paired.append(
            pass_on(
                cross_other, cross, owner,
                core_send.at[len(chunks), slot], core_recv.at[len(chunks), slot], sibling,
            )
        )

    for n, (begin, count, _) in enumerate(chunks):
        turned[n][0].wait_recv()
        arrived(n, depth, z * 2 + 1 - y)
        for d in range(1, depth):
            along[n][d].wait_recv()
            owner = lax.rem(z + depth - d, depth) * 2 + y
            turned[n][d] = pass_on(
                begin, count, owner, y_send.at[n, d], y_recv.at[n, d], beside
            )
            arrived(n, d, owner)
        if n == 0:
            continue
        for d in range(1, depth):
            turned[n - 1][d].wait_recv()
            arrived(n - 1, depth + d, lax.rem(z + depth - d, depth) * 2 + 1 - y)
    for _ in range(depth):
        from_across()
    for d in range(1, depth):
        turned[-1][d].wait_recv()
        arrived(len(chunks) - 1, depth + d, lax.rem(z + depth - d, depth) * 2 + 1 - y)
    while crossed:
        from_across()
    for copy in paired:
        copy.wait_recv()
    for copy in started:
        copy.wait_send()
    for store in stores:
        store.wait()


def finish_kernel(*refs):
    count = (len(refs) - 2) // 3
    load_sem, store_sem = refs[-2:]
    loads, stores = [], []
    for i in range(count):
        source, result, held = refs[i], refs[count + i], refs[2 * count + i]
        rows = source.shape[0] // FINISH_PARTS
        for n in range(FINISH_PARTS):
            block = pl.ds(n * rows, rows)
            loads.append(
                pltpu.make_async_copy(source.at[block], held.at[block], load_sem.at[i, n])
            )
            stores.append(
                pltpu.make_async_copy(held.at[block], result.at[block], store_sem.at[i, n])
            )
    for load in loads:
        load.start()
    for load, store in zip(loads, stores):
        load.wait()
        store.start()
    for store in stores:
        store.wait()


FINISH_PARTS = 4


def kernel_local(shards, reps, *args):
    params = args[13]
    experts, own_channels, parts, channels = params.shape
    planes, depth, devices = reps // 2, shards // 2, shards * reps
    f32, bf16, i32 = jnp.float32, jnp.bfloat16, jnp.int32
    dma = pltpu.SemaphoreType.DMA
    anywhere = pl.BlockSpec(memory_space=pl.ANY)
    vmem = pl.BlockSpec(memory_space=pltpu.VMEM)
    systems, lanes = args[2].shape
    gains = args[10:13]
    tags = gains[0].shape[0] * gains[1].shape[0] * gains[2].shape[0]
    slice_rows = tags * 8
    rows = own_channels * parts
    states = [a.reshape(experts, reps, 8, channels) for a in args[13:16]]
    state = (experts, reps, 8, channels)
    norm_limit = math.sqrt(experts * parts * channels * channels)
    chunk_total = 2

    def held(array):
        return pltpu.VMEM(array.shape, array.dtype)

    def pairs(*shape):
        return [dma(shape), dma(shape)]

    outs = [jax.ShapeDtypeStruct(state, f32)] * 3
    outs.append(jax.ShapeDtypeStruct((experts, shards * rows, channels), bf16))
    results = pl.pallas_call(
        functools.partial(whole_kernel, shards, reps, norm_limit),
        out_shape=outs,
        in_specs=[anywhere] * 16,
        out_specs=[anywhere] * 3 + [vmem],
        scratch_shapes=[
            held(args[0]), held(args[1]), held(args[2]), held(args[5]), held(args[6]),
            *[held(a) for a in gains],
            *[pltpu.VMEM(state, f32)] * 6,
            pltpu.VMEM((tags, 128), f32),
            *[pltpu.SMEM((systems,), i32)] * 5,
            pltpu.SMEM((tags, 128), f32),
            pltpu.VMEM((systems, channels * parts, channels), f32),
            pltpu.VMEM((2, planes, shards, slice_rows, channels), f32),
            pltpu.VMEM((planes, shards, slice_rows, channels), f32),
            pltpu.VMEM((planes, shards, slice_rows, channels), f32),
            pltpu.VMEM((depth, planes * 2 - 1, slice_rows, channels), f32),
            pltpu.VMEM((depth, slice_rows, channels), f32),
            pltpu.VMEM((depth, slice_rows, channels), f32),
            pltpu.VMEM((reps, tags, 8, channels), f32),
            pltpu.VMEM((devices, 8, channels), f32),
            dma((16,)),
            dma((3,)),
            dma,
            dma((2, depth)),
            *pairs(depth, planes * 2 - 1),
            *pairs(depth),
            *pairs(reps),
            *pairs(devices),
            *pairs(chunk_total, depth),
            *pairs(chunk_total, depth),
            *pairs(shards),
            *pairs(chunk_total + 1, shards),
        ],
        compiler_params=pltpu.CompilerParams(
            collective_id=0, has_side_effects=True, vmem_limit_bytes=60 * MIB
        ),
        name="whole",
    )(*args[:13], *states)

    outs = pl.pallas_call(
        finish_kernel,
        out_shape=outs,
        in_specs=[anywhere] * 4,
        out_specs=[anywhere] * 4,
        scratch_shapes=[*[held(a) for a in outs], *pairs(4, FINISH_PARTS)],
        compiler_params=pltpu.CompilerParams(vmem_limit_bytes=60 * MIB),
        name="finish",
    )(*results)
    local_states = [a.reshape(params.shape) for a in outs[:3]]
    return (*local_states, outs[3].reshape(experts, shards * own_channels, parts, channels))


def solution(mesh):
    placed = (
        P(("shard", "rep"), None, None),
        P(("shard", "rep"), None, None),
        P(("shard", "rep"), None),
        P(("shard", "rep")),
        P(("shard", "rep")),
        P(("shard", "rep"), None),
        P(("shard", "rep"), None),
        P(("shard", "rep")),
        P(("shard", "rep")),
        P(("shard", "rep")),
        P(),
        P(),
        P(),
        P(None, "shard", None, None),
        P(None, "shard", None, None),
        P(None, "shard", None, None),
    )
    shards, reps = mesh.shape["shard"], mesh.shape["rep"]

    def local(*args):
        params = args[13]
        if reps == 4 and shards % 2 == 0 and params.shape[1] * params.shape[2] == 8 * reps:
            return kernel_local(shards, reps, *args)
        return plain_local(*args)

    return jax.shard_map(
        local,
        mesh=mesh,
        in_specs=placed,
        out_specs=(
            P(None, "shard", None, None),
            P(None, "shard", None, None),
            P(None, "shard", None, None),
            P(),
        ),
        check_vma=False,
    )
```

```python
import functools
import math

import jax
import jax.numpy as jnp
from jax import lax
from jax.experimental import pallas as pl
from jax.experimental.pallas import tpu as pltpu
from jax.sharding import PartitionSpec as P

STEP = 10


beta_one = 0.9
beta_two = 0.999
adam_eps = 1e-08
learn_rate = 0.01
decay_rate = 0.01
cutoff_radius = 6.0


def envelope(length):
    ratio = length / cutoff_radius
    return 1.0 - 21.0 * ratio**5 + 35.0 * ratio**6 - 15.0 * ratio**7


def mixing_table(dataset_gain, charge_gain, spin_gain):
    product_table = (
        dataset_gain[:, None, None, :] * charge_gain[None, :, None, :] * spin_gain[None, None, :, :]
    )
    product_table = product_table.reshape(-1, product_table.shape[-1])
    return product_table / jnp.sum(product_table, axis=1, keepdims=True)


def onehot_rows(dataset_tag, charge_tag, spin_tag, charge_count, spin_count, row_total):
    tag_rows = (dataset_tag * charge_count + charge_tag) * spin_count + spin_tag
    return (tag_rows[:, None] == jnp.arange(row_total, dtype=jnp.int32)[None, :]).astype(
        jnp.float32
    )


def select_rows(node_rows, slot_ids):
    atom_ids = lax.broadcasted_iota(jnp.int32, (1, node_rows.shape[0]), 1)
    selector = (slot_ids[:, None] == atom_ids).astype(jnp.bfloat16)
    return jnp.dot(selector, node_rows, preferred_element_type=jnp.float32)


def system_product(items):
    feat_rows, cot_rows, length_row, atoms_here, edges_here, source_row, target_row = items
    atom_slots = feat_rows.shape[0]
    edge_input = (select_rows(feat_rows, source_row) * envelope(length_row)[:, None]).astype(
        jnp.bfloat16
    )
    slot_index = lax.broadcasted_iota(jnp.int32, source_row.shape, 0)
    live_mask = (slot_index < edges_here).astype(jnp.float32)
    factor = live_mask * (float(atom_slots) / atoms_here.astype(jnp.float32))
    edge_grad = (select_rows(cot_rows, target_row) * factor[:, None]).astype(jnp.bfloat16)
    return lax.dot_general(
        edge_input, edge_grad, (((0,), (0,)), ((), ())), preferred_element_type=jnp.float32
    )


def adam_update(gradients, params, moment_one, moment_two, square_sum, norm_limit):
    clip_factor = jnp.minimum(1.0, norm_limit / (jnp.sqrt(square_sum) + 1e-06))
    clipped = clip_factor * gradients
    new_one = beta_one * moment_one + (1.0 - beta_one) * clipped
    new_two = beta_two * moment_two + (1.0 - beta_two) * clipped * clipped
    first_fix = 1.0 - beta_one**STEP
    second_fix = 1.0 - beta_two**STEP
    direction = new_one / first_fix / (jnp.sqrt(new_two / second_fix) + adam_eps)
    new_params = params - learn_rate * (direction + decay_rate * params)
    return (new_params, new_one, new_two)


def plain_local(
    node_feat,
    node_cot,
    edge_length,
    atom_count,
    edge_count,
    edge_source,
    edge_target,
    dataset_tag,
    charge_tag,
    spin_tag,
    dataset_gain,
    charge_gain,
    spin_gain,
    params,
    moment_one,
    moment_two,
):
    channels = node_feat.shape[2] // 2
    mixing = mixing_table(dataset_gain, charge_gain, spin_gain)
    tag_onehot = onehot_rows(
        dataset_tag, charge_tag, spin_tag, charge_gain.shape[0], spin_gain.shape[0], mixing.shape[0]
    )
    products = lax.map(
        system_product,
        (node_feat, node_cot, edge_length, atom_count, edge_count, edge_source, edge_target),
    )
    real_part = products[:, :channels, :channels] + products[:, channels:, channels:]
    imag_part = products[:, :channels, channels:] - products[:, channels:, :channels]
    system_grad = jnp.stack([real_part, imag_part], axis=2)
    local_term = jnp.einsum(
        "sk,scto->ckto", tag_onehot, system_grad, precision=lax.Precision.HIGHEST
    )
    summed = lax.psum_scatter(local_term, "shard", scatter_dimension=0, tiled=True)
    summed = lax.psum(summed, "rep")
    gradients = jnp.einsum("ke,ckto->ecto", mixing, summed, precision=lax.Precision.HIGHEST)
    square_sum = lax.psum(jnp.sum(gradients * gradients), "shard")
    norm_limit = math.sqrt(mixing.shape[1] * 2 * channels * channels)
    new_params, new_one, new_two = adam_update(
        gradients, params, moment_one, moment_two, square_sum, norm_limit
    )
    full_weights = lax.all_gather(new_params.astype(jnp.bfloat16), "shard", axis=1, tiled=True)
    return (new_params, new_one, new_two, full_weights)


MIB = 1024 * 1024
MESH = pl.DeviceIdType.MESH


def split_dot(left, right, contract):
    high = right.astype(jnp.bfloat16)
    low = (right - high.astype(jnp.float32)).astype(jnp.bfloat16)
    dims = (contract, ((), ()))
    return lax.dot_general(
        left, high, dims, preferred_element_type=jnp.float32
    ) + lax.dot_general(left, low, dims, preferred_element_type=jnp.float32)


def split_dot_left(left, right):
    high = left.astype(jnp.bfloat16)
    low = (left - high.astype(jnp.float32)).astype(jnp.bfloat16)
    dims = (((0,), (0,)), ((), ()))
    return lax.dot_general(
        high, right, dims, preferred_element_type=jnp.float32
    ) + lax.dot_general(low, right, dims, preferred_element_type=jnp.float32)


def expert_rows(mixing, summed, expert):
    total = mixing[0, expert] * summed[:, 0]
    for k in range(1, summed.shape[1]):
        total = total + mixing[k, expert] * summed[:, k]
    return total


def adam_rows(gradient, clip, params, moment_one, moment_two):
    clipped = clip * gradient
    new_one = beta_one * moment_one + (1.0 - beta_one) * clipped
    new_two = beta_two * moment_two + (1.0 - beta_two) * clipped * clipped
    first_fix = 1.0 - beta_one**STEP
    second_fix = 1.0 - beta_two**STEP
    direction = new_one / first_fix / (jnp.sqrt(new_two / second_fix) + adam_eps)
    return params - learn_rate * (direction + decay_rate * params), new_one, new_two


def system_sums(feat, cot, weight, source, target, atoms, edges, products):
    systems, slots, width = feat.shape
    channels = width // 2
    lanes = source.shape[1]

    def one_system(s, carry):
        slot_index = lax.broadcasted_iota(jnp.int32, (1, lanes), 1)
        atom_index = lax.broadcasted_iota(jnp.int32, (slots, lanes), 0)
        count = jnp.full((1, lanes), atoms[s], jnp.int32).astype(jnp.float32)
        factor = jnp.where(slot_index < edges[s], float(slots) / count, 0.0)
        row = weight[pl.ds(s, 1), :] * factor
        left = jnp.where(atom_index == source[pl.ds(s, 1), :], row, 0.0).astype(jnp.bfloat16)
        right = jnp.where(atom_index == target[pl.ds(s, 1), :], 1.0, 0.0).astype(jnp.bfloat16)
        pairs = lax.dot_general(
            right, left, (((1,), (1,)), ((), ())), preferred_element_type=jnp.float32
        )
        mixed = split_dot_left(pairs, cot[s])
        real, imag = mixed[:, :channels], mixed[:, channels:]
        block = jnp.concatenate(
            [
                jnp.concatenate([real, imag], axis=1),
                jnp.concatenate([imag, -real], axis=1),
            ],
            axis=0,
        )
        rows = feat[s]
        stacked = jnp.concatenate([rows[:, :channels], rows[:, channels:]], axis=0)
        product = split_dot(stacked, block, ((0,), (0,)))
        products[s, pl.ds(0, channels, stride=2), :] = product[:, :channels]
        products[s, pl.ds(1, channels, stride=2), :] = product[:, channels:]
        return carry

    lax.fori_loop(0, systems, one_system, 0, unroll=UNROLL_SYSTEMS)


UNROLL_SYSTEMS = 4
CROSS_PARTS = 2


def whole_kernel(
    shards, reps, norm_limit,
    feat_in, cot_in, length_in, atoms_in, edges_in, source_in, target_in,
    dataset_in, charge_in, spin_in, dataset_gain_in, charge_gain_in, spin_gain_in,
    params_in, one_in, two_in,
    new_params_out, new_one_out, new_two_out, weights,
    feat, cot, length, source, target, dataset_gain, charge_gain, spin_gain,
    params, moment_one, moment_two, new_params, new_one, new_two, table, atoms, edges, dataset, charge, spin, mixing,
    products, pieces, pair_in, pair_sum, slices, z_sum, z_in, summed, norms,
    fetch_sem, store_sem, table_sem, pair_sem, slice_send, slice_recv, ahead_send, ahead_recv, rep_send, rep_recv,
    norm_send, norm_recv, z_send, z_recv, y_send, y_recv, x_send, x_recv, core_send, core_recv,
):
    shard, rep = lax.axis_index("shard"), lax.axis_index("rep")
    planes, depth = reps // 2, shards // 2
    x, core = rep // 2, rep % 2
    z, y = shard // 2, shard % 2
    devices = shards * reps
    me = shard * reps + rep
    experts = params.shape[0]
    tags = summed.shape[1]

    fetches = [
        pltpu.make_async_copy(src, dst, fetch_sem.at[i])
        for i, (src, dst) in enumerate(
            (
                (source_in, source), (target_in, target), (length_in, length),
                (atoms_in, atoms), (edges_in, edges), (cot_in, cot), (feat_in, feat),
                (dataset_in, dataset), (charge_in, charge), (spin_in, spin),
                (dataset_gain_in, dataset_gain), (charge_gain_in, charge_gain),
                (spin_gain_in, spin_gain),
                (params_in, params), (one_in, moment_one), (two_in, moment_two),
            )
        )
    ]
    for fetch in fetches:
        fetch.start()

    barrier = pltpu.get_barrier_semaphore()
    for j in range(1, devices):
        other = lax.rem(me + j, devices)
        pl.semaphore_signal(
            barrier, inc=1, device_id=(other // reps, lax.rem(other, reps)), device_id_type=MESH
        )

    for fetch in fetches[:13]:
        fetch.wait()
    charges, spins = charge_gain.shape[0], spin_gain.shape[0]
    table[...] = jnp.zeros_like(table)
    for k in range(tags):
        d, c, s = k // (charges * spins), (k // spins) % charges, k % spins
        line = dataset_gain[d : d + 1, :] * charge_gain[c : c + 1, :] * spin_gain[s : s + 1, :]
        table[k : k + 1, 0:experts] = line / jnp.sum(line, axis=1, keepdims=True)
    to_scalars = pltpu.make_async_copy(table, mixing, table_sem)
    to_scalars.start()

    length[...] = envelope(length[...])
    system_sums(feat, cot, length, source, target, atoms, edges, products)

    systems, _, channels = products.shape
    rows_of = [
        (dataset[s] * charges + charge[s]) * spins + spin[s] for s in range(systems)
    ]
    takes = [
        [jnp.where(rows_of[s] == k, 1.0, 0.0) for s in range(systems)] for k in range(tags)
    ]

    def group(i, carry):
        at = pl.multiple_of(i * 8, 8)
        terms = [products[s, pl.ds(at, 8), :] for s in range(systems)]
        sums = []
        for k in range(tags):
            total = takes[k][0] * terms[0]
            for s in range(1, systems):
                total = total + takes[k][s] * terms[s]
            sums.append(total)
        owner, r = i // reps, lax.rem(i, reps)
        pieces[lax.rem(r, 2), r // 2, owner] = jnp.concatenate(sums, axis=0)
        return carry

    lax.fori_loop(0, devices, group, 0, unroll=2)
    pl.semaphore_wait(barrier, devices - 1)

    def send(src, dst, send_sem, recv_sem, to):
        copy = pltpu.make_async_remote_copy(
            src_ref=src, dst_ref=dst, send_sem=send_sem, recv_sem=recv_sem,
            device_id=to, device_id_type=MESH,
        )
        copy.start()
        return copy

    sibling = (shard, x * 2 + 1 - core)
    started = []

    parts = [(dz, lax.rem(z + dz, depth)) for dz in [*range(1, depth), 0]]
    sides = [(dx, dy) for dx in range(planes) for dy in range(2) if (dx, dy) != (0, 0)]
    pair, sided, ahead = {}, {}, []
    for dz, to_z in parts:
        both = pl.ds(pl.multiple_of(to_z * 2, 2), 2)
        pair[dz] = send(
            pieces.at[1 - core, :, both], pair_in.at[:, both],
            pair_sem.at[0, dz], pair_sem.at[1, dz], sibling,
        )
    for dz, to_z in parts:
        both = pl.ds(pl.multiple_of(to_z * 2, 2), 2)
        pair[dz].wait_recv()
        pair_sum[:, both] = pieces[core, :, both] + pair_in[:, both]
        for n, (dx, dy) in enumerate(sides):
            to_x, to_y = lax.rem(x + dx, planes), lax.rem(y + dy, 2)
            sided[dz, n] = send(
                pair_sum.at[to_x, to_z * 2 + to_y], slices.at[dz, n],
                slice_send.at[dz, n], slice_recv.at[dz, n],
                (z * 2 + to_y, to_x * 2 + core),
            )
    for dz, to_z in parts:
        total = pair_sum[x, to_z * 2 + y]
        for n in range(len(sides)):
            sided[dz, n].wait_recv()
            total = total + slices[dz, n]
        if dz > 0:
            z_sum[dz] = total
            ahead.append(
                send(
                    z_sum.at[dz], z_in.at[dz], ahead_send.at[dz], ahead_recv.at[dz],
                    (to_z * 2 + y, rep),
                )
            )
    to_scalars.wait()
    for n, copy in enumerate(ahead):
        copy.wait_recv()
        total = total + z_in[n + 1]
    started += [*pair.values(), *sided.values(), *ahead]
    own = total.reshape(tags, 8, total.shape[-1])
    summed[rep] = own

    shared = []
    for j in range(1, reps):
        shared.append(
            send(
                summed.at[rep], summed.at[rep], rep_send.at[j], rep_recv.at[j],
                (shard, lax.rem(rep + j, reps)),
            )
        )
    squares = jnp.zeros(own.shape[1:], jnp.float32)
    for e in range(experts):
        gradient = expert_rows(mixing, own[None], e)[0]
        squares = squares + gradient * gradient
    norms[me] = squares
    normed = []
    for j in range(1, devices):
        other = lax.rem(me + j, devices)
        normed.append(
            send(
                norms.at[me], norms.at[me], norm_send.at[j], norm_recv.at[j],
                (other // reps, lax.rem(other, reps)),
            )
        )
    for fetch in fetches[13:]:
        fetch.wait()
    for copy in shared:
        copy.wait_recv()
    for copy in normed:
        copy.wait_recv()
    started += shared + normed
    square_sum = jnp.sum(jnp.sum(norms[...], axis=0), axis=(0, 1), keepdims=True)
    clip = jnp.minimum(1.0, norm_limit / (jnp.sqrt(square_sum) + 1e-06))

    half = experts // 2
    span = (half * 5) // 8
    cross = half - span
    first = core * half + x * cross
    part = cross // CROSS_PARTS
    chunks = [
        (core * half + x * span + n * part, part, True) for n in range(CROSS_PARTS)
    ] + [(core * half + cross, span - cross, False)]
    cross_other = core * half + (1 - x) * span
    rows = weights.shape[1] // shards

    def update(begin):
        def one(i, carry):
            e = lax.rem(begin + i, experts)
            new_params[e], new_one[e], new_two[e] = adam_rows(
                expert_rows(mixing, summed, e), clip, params[e], moment_one[e], moment_two[e]
            )
            weights[e, pl.ds(pl.multiple_of(shard * rows, rows), rows), :] = (
                new_params[e].reshape(rows, weights.shape[-1]).astype(jnp.bfloat16)
            )
            return carry

        return one

    def pass_on(begin, count, owner, send_sem, recv_sem, to):
        block = weights.at[
            pl.ds(begin, count), pl.ds(pl.multiple_of(owner * rows, rows), rows), :
        ]
        copy = send(block, block, send_sem, recv_sem, to)
        started.append(copy)
        return copy

    beside = (z * 2 + 1 - y, rep)
    across = (shard, (1 - x) * 2 + core)
    along = [[None] * depth for _ in chunks]
    turned = [[None] * depth for _ in chunks]
    for n, (begin, count, _) in enumerate(chunks):
        lax.fori_loop(0, count, update(begin), 0, unroll=count)
        for d in range(1, depth):
            to = lax.rem(z + d, depth) * 2 + y
            along[n][d] = pass_on(
                begin, count, shard, z_send.at[n, d], z_recv.at[n, d], (to, rep)
            )
        turned[n][0] = pass_on(begin, count, shard, y_send.at[n, 0], y_recv.at[n, 0], beside)
    lax.fori_loop(0, experts - span, update(first + span), 0, unroll=2)
    stores = [
        pltpu.make_async_copy(src, dst, store_sem.at[i])
        for i, (src, dst) in enumerate(
            ((new_params, new_params_out), (new_one, new_one_out), (new_two, new_two_out))
        )
    ]
    for store in stores:
        store.start()

    crossed, paired = [[] for _ in range(shards)], []
    last = len(chunks) - 1

    def arrived(n, slot, owner):
        begin, count, crosses = chunks[n]
        if crosses:
            copy = pass_on(begin, count, owner, x_send.at[n, slot], x_recv.at[n, slot], across)
            crossed[slot].append(copy)
        if n == last:
            paired.append(
                pass_on(first, span, owner, core_send.at[0, slot], core_recv.at[0, slot], sibling)
            )

    def from_across(slot, owner):
        for copy in crossed[slot]:
            copy.wait_recv()
        paired.append(
            pass_on(
                cross_other, cross, owner, core_send.at[1, slot], core_recv.at[1, slot], sibling
            )
        )

    def owner_at(d, side):
        return lax.rem(z + depth - d, depth) * 2 + (y if side == 0 else 1 - y)

    def turned_in(n):
        for d in range(1, depth):
            turned[n][d].wait_recv()
            arrived(n, depth + d, owner_at(d, 1))

    for n, (begin, count, _) in enumerate(chunks):
        turned[n][0].wait_recv()
        arrived(n, depth, owner_at(0, 1))
        for d in range(1, depth):
            along[n][d].wait_recv()
            turned[n][d] = pass_on(
                begin, count, owner_at(d, 0), y_send.at[n, d], y_recv.at[n, d], beside
            )
            arrived(n, d, owner_at(d, 0))
        if n > 0:
            turned_in(n - 1)
    from_across(depth, owner_at(0, 1))
    for d in range(1, depth):
        from_across(d, owner_at(d, 0))
    turned_in(last)
    for d in range(1, depth):
        from_across(depth + d, owner_at(d, 1))
    for copy in paired:
        copy.wait_recv()
    for copy in started:
        copy.wait_send()
    for store in stores:
        store.wait()


def finish_kernel(*refs):
    count = (len(refs) - 2) // 3
    load_sem, store_sem = refs[-2:]
    loads, stores = [], []
    for i in range(count):
        source, result, held = refs[i], refs[count + i], refs[2 * count + i]
        rows = source.shape[0] // FINISH_PARTS
        for n in range(FINISH_PARTS):
            block = pl.ds(n * rows, rows)
            loads.append(
                pltpu.make_async_copy(source.at[block], held.at[block], load_sem.at[i, n])
            )
            stores.append(
                pltpu.make_async_copy(held.at[block], result.at[block], store_sem.at[i, n])
            )
    for load in loads:
        load.start()
    for load, store in zip(loads, stores):
        load.wait()
        store.start()
    for store in stores:
        store.wait()


FINISH_PARTS = 4


def kernel_local(shards, reps, *args):
    params = args[13]
    experts, own_channels, parts, channels = params.shape
    planes, depth, devices = reps // 2, shards // 2, shards * reps
    f32, bf16, i32 = jnp.float32, jnp.bfloat16, jnp.int32
    dma = pltpu.SemaphoreType.DMA
    anywhere = pl.BlockSpec(memory_space=pl.ANY)
    vmem = pl.BlockSpec(memory_space=pltpu.VMEM)
    systems, lanes = args[2].shape
    gains = args[10:13]
    tags = gains[0].shape[0] * gains[1].shape[0] * gains[2].shape[0]
    slice_rows = tags * 8
    rows = own_channels * parts
    states = [a.reshape(experts, reps, 8, channels) for a in args[13:16]]
    state = (experts, reps, 8, channels)
    norm_limit = math.sqrt(experts * parts * channels * channels)
    chunk_total = CROSS_PARTS + 1

    def held(array):
        return pltpu.VMEM(array.shape, array.dtype)

    def pairs(*shape):
        return [dma(shape), dma(shape)]

    outs = [jax.ShapeDtypeStruct(state, f32)] * 3
    outs.append(jax.ShapeDtypeStruct((experts, shards * rows, channels), bf16))
    results = pl.pallas_call(
        functools.partial(whole_kernel, shards, reps, norm_limit),
        out_shape=outs,
        in_specs=[anywhere] * 16,
        out_specs=[anywhere] * 3 + [vmem],
        scratch_shapes=[
            held(args[0]), held(args[1]), held(args[2]), held(args[5]), held(args[6]),
            *[held(a) for a in gains],
            *[pltpu.VMEM(state, f32)] * 6,
            pltpu.VMEM((tags, 128), f32),
            *[pltpu.SMEM((systems,), i32)] * 5,
            pltpu.SMEM((tags, 128), f32),
            pltpu.VMEM((systems, channels * parts, channels), f32),
            pltpu.VMEM((2, planes, shards, slice_rows, channels), f32),
            pltpu.VMEM((planes, shards, slice_rows, channels), f32),
            pltpu.VMEM((planes, shards, slice_rows, channels), f32),
            pltpu.VMEM((depth, planes * 2 - 1, slice_rows, channels), f32),
            pltpu.VMEM((depth, slice_rows, channels), f32),
            pltpu.VMEM((depth, slice_rows, channels), f32),
            pltpu.VMEM((reps, tags, 8, channels), f32),
            pltpu.VMEM((devices, 8, channels), f32),
            dma((16,)),
            dma((3,)),
            dma,
            dma((2, depth)),
            *pairs(depth, planes * 2 - 1),
            *pairs(depth),
            *pairs(reps),
            *pairs(devices),
            *pairs(chunk_total, depth),
            *pairs(chunk_total, depth),
            *pairs(CROSS_PARTS, shards),
            *pairs(2, shards),
        ],
        compiler_params=pltpu.CompilerParams(
            collective_id=0, has_side_effects=True, vmem_limit_bytes=60 * MIB
        ),
        name="whole",
    )(*args[:13], *states)

    outs = pl.pallas_call(
        finish_kernel,
        out_shape=outs,
        in_specs=[anywhere] * 4,
        out_specs=[anywhere] * 4,
        scratch_shapes=[*[held(a) for a in outs], *pairs(4, FINISH_PARTS)],
        compiler_params=pltpu.CompilerParams(vmem_limit_bytes=60 * MIB),
        name="finish",
    )(*results)
    local_states = [a.reshape(params.shape) for a in outs[:3]]
    return (*local_states, outs[3].reshape(experts, shards * own_channels, parts, channels))


def solution(mesh):
    placed = (
        P(("shard", "rep"), None, None),
        P(("shard", "rep"), None, None),
        P(("shard", "rep"), None),
        P(("shard", "rep")),
        P(("shard", "rep")),
        P(("shard", "rep"), None),
        P(("shard", "rep"), None),
        P(("shard", "rep")),
        P(("shard", "rep")),
        P(("shard", "rep")),
        P(),
        P(),
        P(),
        P(None, "shard", None, None),
        P(None, "shard", None, None),
        P(None, "shard", None, None),
    )
    shards, reps = mesh.shape["shard"], mesh.shape["rep"]

    def local(*args):
        params = args[13]
        if reps == 4 and shards % 2 == 0 and params.shape[1] * params.shape[2] == 8 * reps:
            return kernel_local(shards, reps, *args)
        return plain_local(*args)

    return jax.shard_map(
        local,
        mesh=mesh,
        in_specs=placed,
        out_specs=(
            P(None, "shard", None, None),
            P(None, "shard", None, None),
            P(None, "shard", None, None),
            P(),
        ),
        check_vma=False,
    )
```

```python
import functools
import math

import jax
import jax.numpy as jnp
from jax import lax
from jax.experimental import pallas as pl
from jax.experimental.pallas import tpu as pltpu
from jax.sharding import PartitionSpec as P

STEP = 10


beta_one = 0.9
beta_two = 0.999
adam_eps = 1e-08
learn_rate = 0.01
decay_rate = 0.01
cutoff_radius = 6.0


def envelope(length):
    ratio = length / cutoff_radius
    return 1.0 - 21.0 * ratio**5 + 35.0 * ratio**6 - 15.0 * ratio**7


def mixing_table(dataset_gain, charge_gain, spin_gain):
    product_table = (
        dataset_gain[:, None, None, :] * charge_gain[None, :, None, :] * spin_gain[None, None, :, :]
    )
    product_table = product_table.reshape(-1, product_table.shape[-1])
    return product_table / jnp.sum(product_table, axis=1, keepdims=True)


def onehot_rows(dataset_tag, charge_tag, spin_tag, charge_count, spin_count, row_total):
    tag_rows = (dataset_tag * charge_count + charge_tag) * spin_count + spin_tag
    return (tag_rows[:, None] == jnp.arange(row_total, dtype=jnp.int32)[None, :]).astype(
        jnp.float32
    )


def select_rows(node_rows, slot_ids):
    atom_ids = lax.broadcasted_iota(jnp.int32, (1, node_rows.shape[0]), 1)
    selector = (slot_ids[:, None] == atom_ids).astype(jnp.bfloat16)
    return jnp.dot(selector, node_rows, preferred_element_type=jnp.float32)


def system_product(items):
    feat_rows, cot_rows, length_row, atoms_here, edges_here, source_row, target_row = items
    atom_slots = feat_rows.shape[0]
    edge_input = (select_rows(feat_rows, source_row) * envelope(length_row)[:, None]).astype(
        jnp.bfloat16
    )
    slot_index = lax.broadcasted_iota(jnp.int32, source_row.shape, 0)
    live_mask = (slot_index < edges_here).astype(jnp.float32)
    factor = live_mask * (float(atom_slots) / atoms_here.astype(jnp.float32))
    edge_grad = (select_rows(cot_rows, target_row) * factor[:, None]).astype(jnp.bfloat16)
    return lax.dot_general(
        edge_input, edge_grad, (((0,), (0,)), ((), ())), preferred_element_type=jnp.float32
    )


def adam_update(gradients, params, moment_one, moment_two, square_sum, norm_limit):
    clip_factor = jnp.minimum(1.0, norm_limit / (jnp.sqrt(square_sum) + 1e-06))
    clipped = clip_factor * gradients
    new_one = beta_one * moment_one + (1.0 - beta_one) * clipped
    new_two = beta_two * moment_two + (1.0 - beta_two) * clipped * clipped
    first_fix = 1.0 - beta_one**STEP
    second_fix = 1.0 - beta_two**STEP
    direction = new_one / first_fix / (jnp.sqrt(new_two / second_fix) + adam_eps)
    new_params = params - learn_rate * (direction + decay_rate * params)
    return (new_params, new_one, new_two)


def plain_local(
    node_feat,
    node_cot,
    edge_length,
    atom_count,
    edge_count,
    edge_source,
    edge_target,
    dataset_tag,
    charge_tag,
    spin_tag,
    dataset_gain,
    charge_gain,
    spin_gain,
    params,
    moment_one,
    moment_two,
):
    channels = node_feat.shape[2] // 2
    mixing = mixing_table(dataset_gain, charge_gain, spin_gain)
    tag_onehot = onehot_rows(
        dataset_tag, charge_tag, spin_tag, charge_gain.shape[0], spin_gain.shape[0], mixing.shape[0]
    )
    products = lax.map(
        system_product,
        (node_feat, node_cot, edge_length, atom_count, edge_count, edge_source, edge_target),
    )
    real_part = products[:, :channels, :channels] + products[:, channels:, channels:]
    imag_part = products[:, :channels, channels:] - products[:, channels:, :channels]
    system_grad = jnp.stack([real_part, imag_part], axis=2)
    local_term = jnp.einsum(
        "sk,scto->ckto", tag_onehot, system_grad, precision=lax.Precision.HIGHEST
    )
    summed = lax.psum_scatter(local_term, "shard", scatter_dimension=0, tiled=True)
    summed = lax.psum(summed, "rep")
    gradients = jnp.einsum("ke,ckto->ecto", mixing, summed, precision=lax.Precision.HIGHEST)
    square_sum = lax.psum(jnp.sum(gradients * gradients), "shard")
    norm_limit = math.sqrt(mixing.shape[1] * 2 * channels * channels)
    new_params, new_one, new_two = adam_update(
        gradients, params, moment_one, moment_two, square_sum, norm_limit
    )
    full_weights = lax.all_gather(new_params.astype(jnp.bfloat16), "shard", axis=1, tiled=True)
    return (new_params, new_one, new_two, full_weights)


MIB = 1024 * 1024
MESH = pl.DeviceIdType.MESH


def split_dot(left, right, contract):
    high = right.astype(jnp.bfloat16)
    low = (right - high.astype(jnp.float32)).astype(jnp.bfloat16)
    dims = (contract, ((), ()))
    return lax.dot_general(
        left, high, dims, preferred_element_type=jnp.float32
    ) + lax.dot_general(left, low, dims, preferred_element_type=jnp.float32)


def split_dot_left(left, right):
    high = left.astype(jnp.bfloat16)
    low = (left - high.astype(jnp.float32)).astype(jnp.bfloat16)
    dims = (((0,), (0,)), ((), ()))
    return lax.dot_general(
        high, right, dims, preferred_element_type=jnp.float32
    ) + lax.dot_general(low, right, dims, preferred_element_type=jnp.float32)


def expert_rows(mixing, summed, expert):
    total = mixing[0, expert] * summed[:, 0]
    for k in range(1, summed.shape[1]):
        total = total + mixing[k, expert] * summed[:, k]
    return total


def adam_rows(gradient, clip, params, moment_one, moment_two):
    clipped = clip * gradient
    new_one = beta_one * moment_one + (1.0 - beta_one) * clipped
    new_two = beta_two * moment_two + (1.0 - beta_two) * clipped * clipped
    first_fix = 1.0 - beta_one**STEP
    second_fix = 1.0 - beta_two**STEP
    direction = new_one / first_fix / (jnp.sqrt(new_two / second_fix) + adam_eps)
    return params - learn_rate * (direction + decay_rate * params), new_one, new_two


def system_sums(feat, cot, weight, source, target, atoms, edges, products):
    systems, slots, width = feat.shape
    channels = width // 2
    lanes = source.shape[1]

    def one_system(s, carry):
        slot_index = lax.broadcasted_iota(jnp.int32, (1, lanes), 1)
        atom_index = lax.broadcasted_iota(jnp.int32, (slots, lanes), 0)
        count = jnp.full((1, lanes), atoms[s], jnp.int32).astype(jnp.float32)
        factor = jnp.where(slot_index < edges[s], float(slots) / count, 0.0)
        row = weight[pl.ds(s, 1), :] * factor
        left = jnp.where(atom_index == source[pl.ds(s, 1), :], row, 0.0).astype(jnp.bfloat16)
        right = jnp.where(atom_index == target[pl.ds(s, 1), :], 1.0, 0.0).astype(jnp.bfloat16)
        pairs = lax.dot_general(
            right, left, (((1,), (1,)), ((), ())), preferred_element_type=jnp.float32
        )
        mixed = split_dot_left(pairs, cot[s])
        real, imag = mixed[:, :channels], mixed[:, channels:]
        block = jnp.concatenate(
            [
                jnp.concatenate([real, imag], axis=1),
                jnp.concatenate([imag, -real], axis=1),
            ],
            axis=0,
        )
        rows = feat[s]
        stacked = jnp.concatenate([rows[:, :channels], rows[:, channels:]], axis=0)
        product = split_dot(stacked, block, ((0,), (0,)))
        products[s, pl.ds(0, channels, stride=2), :] = product[:, :channels]
        products[s, pl.ds(1, channels, stride=2), :] = product[:, channels:]
        return carry

    lax.fori_loop(0, systems, one_system, 0, unroll=UNROLL_SYSTEMS)


UNROLL_SYSTEMS = 4
CROSS_PARTS = 2


def whole_kernel(
    shards, reps, norm_limit,
    feat_in, cot_in, length_in, atoms_in, edges_in, source_in, target_in,
    dataset_in, charge_in, spin_in, dataset_gain_in, charge_gain_in, spin_gain_in,
    params_in, one_in, two_in,
    new_params_out, new_one_out, new_two_out, weights,
    feat, cot, length, source, target, dataset_gain, charge_gain, spin_gain,
    params, moment_one, moment_two, new_params, new_one, new_two, table, atoms, edges, dataset, charge, spin, mixing,
    products, pieces, pair_in, pair_sum, slices, z_sum, z_in, summed, norms,
    fetch_sem, store_sem, table_sem, pair_sem, slice_send, slice_recv, ahead_send, ahead_recv, rep_send, rep_recv,
    norm_send, norm_recv, z_send, z_recv, y_send, y_recv, x_send, x_recv, core_send, core_recv,
):
    shard, rep = lax.axis_index("shard"), lax.axis_index("rep")
    planes, depth = reps // 2, shards // 2
    x, core = rep // 2, rep % 2
    z, y = shard // 2, shard % 2
    devices = shards * reps
    me = shard * reps + rep
    experts = params.shape[0]
    tags = summed.shape[1]

    fetches = [
        pltpu.make_async_copy(src, dst, fetch_sem.at[i])
        for i, (src, dst) in enumerate(
            (
                (source_in, source), (target_in, target), (length_in, length),
                (atoms_in, atoms), (edges_in, edges), (cot_in, cot), (feat_in, feat),
                (dataset_in, dataset), (charge_in, charge), (spin_in, spin),
                (dataset_gain_in, dataset_gain), (charge_gain_in, charge_gain),
                (spin_gain_in, spin_gain),
                (params_in, params), (one_in, moment_one), (two_in, moment_two),
            )
        )
    ]
    for fetch in fetches:
        fetch.start()

    barrier = pltpu.get_barrier_semaphore()
    for j in range(1, devices):
        other = lax.rem(me + j, devices)
        pl.semaphore_signal(
            barrier, inc=1, device_id=(other // reps, lax.rem(other, reps)), device_id_type=MESH
        )

    for fetch in fetches[:13]:
        fetch.wait()
    charges, spins = charge_gain.shape[0], spin_gain.shape[0]
    table[...] = jnp.zeros_like(table)
    for k in range(tags):
        d, c, s = k // (charges * spins), (k // spins) % charges, k % spins
        line = dataset_gain[d : d + 1, :] * charge_gain[c : c + 1, :] * spin_gain[s : s + 1, :]
        table[k : k + 1, 0:experts] = line / jnp.sum(line, axis=1, keepdims=True)
    to_scalars = pltpu.make_async_copy(table, mixing, table_sem)
    to_scalars.start()

    length[...] = envelope(length[...])
    system_sums(feat, cot, length, source, target, atoms, edges, products)

    systems, _, channels = products.shape
    rows_of = [
        (dataset[s] * charges + charge[s]) * spins + spin[s] for s in range(systems)
    ]
    takes = [
        [jnp.where(rows_of[s] == k, 1.0, 0.0) for s in range(systems)] for k in range(tags)
    ]

    block_rows = reps * 8

    def group(owner):
        at = pl.multiple_of(owner * block_rows, block_rows)
        terms = [products[s, pl.ds(at, block_rows), :] for s in range(systems)]
        for k in range(tags):
            total = takes[k][0] * terms[0]
            for s in range(1, systems):
                total = total + takes[k][s] * terms[s]
            for r in range(reps):
                pieces[r % 2, r // 2, owner, 8 * k : 8 * k + 8, :] = total[8 * r : 8 * r + 8, :]

    pl.semaphore_wait(barrier, devices - 1)

    def send(src, dst, send_sem, recv_sem, to):
        copy = pltpu.make_async_remote_copy(
            src_ref=src, dst_ref=dst, send_sem=send_sem, recv_sem=recv_sem,
            device_id=to, device_id_type=MESH,
        )
        copy.start()
        return copy

    sibling = (shard, x * 2 + 1 - core)
    started = []

    parts = [(dz, lax.rem(z + dz, depth)) for dz in [*range(1, depth), 0]]
    sides = [(dx, dy) for dx in range(planes) for dy in range(2) if (dx, dy) != (0, 0)]
    pair, sided, ahead = {}, {}, []
    for dz, to_z in parts:
        both = pl.ds(pl.multiple_of(to_z * 2, 2), 2)
        group(to_z * 2)
        group(to_z * 2 + 1)
        pair[dz] = send(
            pieces.at[1 - core, :, both], pair_in.at[:, both],
            pair_sem.at[0, dz], pair_sem.at[1, dz], sibling,
        )
    for dz, to_z in parts:
        both = pl.ds(pl.multiple_of(to_z * 2, 2), 2)
        pair[dz].wait_recv()
        pair_sum[:, both] = pieces[core, :, both] + pair_in[:, both]
        for n, (dx, dy) in enumerate(sides):
            to_x, to_y = lax.rem(x + dx, planes), lax.rem(y + dy, 2)
            sided[dz, n] = send(
                pair_sum.at[to_x, to_z * 2 + to_y], slices.at[dz, n],
                slice_send.at[dz, n], slice_recv.at[dz, n],
                (z * 2 + to_y, to_x * 2 + core),
            )
    for dz, to_z in parts:
        total = pair_sum[x, to_z * 2 + y]
        for n in range(len(sides)):
            sided[dz, n].wait_recv()
            total = total + slices[dz, n]
        if dz > 0:
            z_sum[dz] = total
            ahead.append(
                send(
                    z_sum.at[dz], z_in.at[dz], ahead_send.at[dz], ahead_recv.at[dz],
                    (to_z * 2 + y, rep),
                )
            )
    to_scalars.wait()
    for n, copy in enumerate(ahead):
        copy.wait_recv()
        total = total + z_in[n + 1]
    started += [*pair.values(), *sided.values(), *ahead]
    own = total.reshape(tags, 8, total.shape[-1])
    summed[rep] = own

    shared = []
    for j in range(1, reps):
        shared.append(
            send(
                summed.at[rep], summed.at[rep], rep_send.at[j], rep_recv.at[j],
                (shard, lax.rem(rep + j, reps)),
            )
        )
    squares = jnp.zeros(own.shape[1:], jnp.float32)
    for e in range(experts):
        gradient = expert_rows(mixing, own[None], e)[0]
        squares = squares + gradient * gradient
    norms[me] = squares
    normed = []
    for j in range(1, devices):
        other = lax.rem(me + j, devices)
        normed.append(
            send(
                norms.at[me], norms.at[me], norm_send.at[j], norm_recv.at[j],
                (other // reps, lax.rem(other, reps)),
            )
        )
    for fetch in fetches[13:]:
        fetch.wait()
    for copy in shared:
        copy.wait_recv()
    for copy in normed:
        copy.wait_recv()
    started += shared + normed
    square_sum = jnp.sum(jnp.sum(norms[...], axis=0), axis=(0, 1), keepdims=True)
    clip = jnp.minimum(1.0, norm_limit / (jnp.sqrt(square_sum) + 1e-06))

    half = experts // 2
    span = (half * 5) // 8
    cross = half - span
    first = core * half + x * cross
    part = cross // CROSS_PARTS
    chunks = [
        (core * half + x * span + n * part, part, True) for n in range(CROSS_PARTS)
    ] + [(core * half + cross, span - cross, False)]
    cross_other = core * half + (1 - x) * span
    rows = weights.shape[1] // shards

    def update(begin):
        def one(i, carry):
            e = lax.rem(begin + i, experts)
            new_params[e], new_one[e], new_two[e] = adam_rows(
                expert_rows(mixing, summed, e), clip, params[e], moment_one[e], moment_two[e]
            )
            weights[e, pl.ds(pl.multiple_of(shard * rows, rows), rows), :] = (
                new_params[e].reshape(rows, weights.shape[-1]).astype(jnp.bfloat16)
            )
            return carry

        return one

    def pass_on(begin, count, owner, send_sem, recv_sem, to):
        block = weights.at[
            pl.ds(begin, count), pl.ds(pl.multiple_of(owner * rows, rows), rows), :
        ]
        copy = send(block, block, send_sem, recv_sem, to)
        started.append(copy)
        return copy

    beside = (z * 2 + 1 - y, rep)
    across = (shard, (1 - x) * 2 + core)
    along = [[None] * depth for _ in chunks]
    turned = [[None] * depth for _ in chunks]
    for n, (begin, count, _) in enumerate(chunks):
        lax.fori_loop(0, count, update(begin), 0, unroll=count)
        for d in range(1, depth):
            to = lax.rem(z + d, depth) * 2 + y
            along[n][d] = pass_on(
                begin, count, shard, z_send.at[n, d], z_recv.at[n, d], (to, rep)
            )
        turned[n][0] = pass_on(begin, count, shard, y_send.at[n, 0], y_recv.at[n, 0], beside)
    lax.fori_loop(0, experts - span, update(first + span), 0, unroll=2)
    stores = [
        pltpu.make_async_copy(src, dst, store_sem.at[i])
        for i, (src, dst) in enumerate(
            ((new_params, new_params_out), (new_one, new_one_out), (new_two, new_two_out))
        )
    ]
    for store in stores:
        store.start()

    crossed, paired = [[] for _ in range(shards)], []
    last = len(chunks) - 1

    def arrived(n, slot, owner):
        begin, count, crosses = chunks[n]
        if crosses:
            copy = pass_on(begin, count, owner, x_send.at[n, slot], x_recv.at[n, slot], across)
            crossed[slot].append(copy)
        if n == last:
            paired.append(
                pass_on(first, span, owner, core_send.at[0, slot], core_recv.at[0, slot], sibling)
            )

    def from_across(slot, owner):
        for copy in crossed[slot]:
            copy.wait_recv()
        paired.append(
            pass_on(
                cross_other, cross, owner, core_send.at[1, slot], core_recv.at[1, slot], sibling
            )
        )

    def owner_at(d, side):
        return lax.rem(z + depth - d, depth) * 2 + (y if side == 0 else 1 - y)

    def turned_in(n):
        for d in range(1, depth):
            turned[n][d].wait_recv()
            arrived(n, depth + d, owner_at(d, 1))

    for n, (begin, count, _) in enumerate(chunks):
        turned[n][0].wait_recv()
        arrived(n, depth, owner_at(0, 1))
        for d in range(1, depth):
            along[n][d].wait_recv()
            turned[n][d] = pass_on(
                begin, count, owner_at(d, 0), y_send.at[n, d], y_recv.at[n, d], beside
            )
            arrived(n, d, owner_at(d, 0))
        if n > 0:
            turned_in(n - 1)
    from_across(depth, owner_at(0, 1))
    for d in range(1, depth):
        from_across(d, owner_at(d, 0))
    turned_in(last)
    for d in range(1, depth):
        from_across(depth + d, owner_at(d, 1))
    for copy in paired:
        copy.wait_recv()
    for copy in started:
        copy.wait_send()
    for store in stores:
        store.wait()


def finish_kernel(*refs):
    count = (len(refs) - 2) // 3
    load_sem, store_sem = refs[-2:]
    loads, stores = [], []
    for i in range(count):
        source, result, held = refs[i], refs[count + i], refs[2 * count + i]
        rows = source.shape[0] // FINISH_PARTS
        for n in range(FINISH_PARTS):
            block = pl.ds(n * rows, rows)
            loads.append(
                pltpu.make_async_copy(source.at[block], held.at[block], load_sem.at[i, n])
            )
            stores.append(
                pltpu.make_async_copy(held.at[block], result.at[block], store_sem.at[i, n])
            )
    for load in loads:
        load.start()
    for load, store in zip(loads, stores):
        load.wait()
        store.start()
    for store in stores:
        store.wait()


FINISH_PARTS = 4


def kernel_local(shards, reps, *args):
    params = args[13]
    experts, own_channels, parts, channels = params.shape
    planes, depth, devices = reps // 2, shards // 2, shards * reps
    f32, bf16, i32 = jnp.float32, jnp.bfloat16, jnp.int32
    dma = pltpu.SemaphoreType.DMA
    anywhere = pl.BlockSpec(memory_space=pl.ANY)
    vmem = pl.BlockSpec(memory_space=pltpu.VMEM)
    systems, lanes = args[2].shape
    gains = args[10:13]
    tags = gains[0].shape[0] * gains[1].shape[0] * gains[2].shape[0]
    slice_rows = tags * 8
    rows = own_channels * parts
    states = [a.reshape(experts, reps, 8, channels) for a in args[13:16]]
    state = (experts, reps, 8, channels)
    norm_limit = math.sqrt(experts * parts * channels * channels)
    chunk_total = CROSS_PARTS + 1

    def held(array):
        return pltpu.VMEM(array.shape, array.dtype)

    def pairs(*shape):
        return [dma(shape), dma(shape)]

    outs = [jax.ShapeDtypeStruct(state, f32)] * 3
    outs.append(jax.ShapeDtypeStruct((experts, shards * rows, channels), bf16))
    results = pl.pallas_call(
        functools.partial(whole_kernel, shards, reps, norm_limit),
        out_shape=outs,
        in_specs=[anywhere] * 16,
        out_specs=[anywhere] * 3 + [vmem],
        scratch_shapes=[
            held(args[0]), held(args[1]), held(args[2]), held(args[5]), held(args[6]),
            *[held(a) for a in gains],
            *[pltpu.VMEM(state, f32)] * 6,
            pltpu.VMEM((tags, 128), f32),
            *[pltpu.SMEM((systems,), i32)] * 5,
            pltpu.SMEM((tags, 128), f32),
            pltpu.VMEM((systems, channels * parts, channels), f32),
            pltpu.VMEM((2, planes, shards, slice_rows, channels), f32),
            pltpu.VMEM((planes, shards, slice_rows, channels), f32),
            pltpu.VMEM((planes, shards, slice_rows, channels), f32),
            pltpu.VMEM((depth, planes * 2 - 1, slice_rows, channels), f32),
            pltpu.VMEM((depth, slice_rows, channels), f32),
            pltpu.VMEM((depth, slice_rows, channels), f32),
            pltpu.VMEM((reps, tags, 8, channels), f32),
            pltpu.VMEM((devices, 8, channels), f32),
            dma((16,)),
            dma((3,)),
            dma,
            dma((2, depth)),
            *pairs(depth, planes * 2 - 1),
            *pairs(depth),
            *pairs(reps),
            *pairs(devices),
            *pairs(chunk_total, depth),
            *pairs(chunk_total, depth),
            *pairs(CROSS_PARTS, shards),
            *pairs(2, shards),
        ],
        compiler_params=pltpu.CompilerParams(
            collective_id=0, has_side_effects=True, vmem_limit_bytes=60 * MIB
        ),
        name="whole",
    )(*args[:13], *states)

    outs = pl.pallas_call(
        finish_kernel,
        out_shape=outs,
        in_specs=[anywhere] * 4,
        out_specs=[anywhere] * 4,
        scratch_shapes=[*[held(a) for a in outs], *pairs(4, FINISH_PARTS)],
        compiler_params=pltpu.CompilerParams(vmem_limit_bytes=60 * MIB),
        name="finish",
    )(*results)
    local_states = [a.reshape(params.shape) for a in outs[:3]]
    return (*local_states, outs[3].reshape(experts, shards * own_channels, parts, channels))


def solution(mesh):
    placed = (
        P(("shard", "rep"), None, None),
        P(("shard", "rep"), None, None),
        P(("shard", "rep"), None),
        P(("shard", "rep")),
        P(("shard", "rep")),
        P(("shard", "rep"), None),
        P(("shard", "rep"), None),
        P(("shard", "rep")),
        P(("shard", "rep")),
        P(("shard", "rep")),
        P(),
        P(),
        P(),
        P(None, "shard", None, None),
        P(None, "shard", None, None),
        P(None, "shard", None, None),
    )
    shards, reps = mesh.shape["shard"], mesh.shape["rep"]

    def local(*args):
        params = args[13]
        if reps == 4 and shards % 2 == 0 and params.shape[1] * params.shape[2] == 8 * reps:
            return kernel_local(shards, reps, *args)
        return plain_local(*args)

    return jax.shard_map(
        local,
        mesh=mesh,
        in_specs=placed,
        out_specs=(
            P(None, "shard", None, None),
            P(None, "shard", None, None),
            P(None, "shard", None, None),
            P(),
        ),
        check_vma=False,
    )
```

```python
import functools
import math

import jax
import jax.numpy as jnp
from jax import lax
from jax.experimental import pallas as pl
from jax.experimental.pallas import tpu as pltpu
from jax.sharding import PartitionSpec as P

STEP = 10


beta_one = 0.9
beta_two = 0.999
adam_eps = 1e-08
learn_rate = 0.01
decay_rate = 0.01
cutoff_radius = 6.0


def envelope(length):
    ratio = length / cutoff_radius
    return 1.0 - 21.0 * ratio**5 + 35.0 * ratio**6 - 15.0 * ratio**7


def mixing_table(dataset_gain, charge_gain, spin_gain):
    product_table = (
        dataset_gain[:, None, None, :] * charge_gain[None, :, None, :] * spin_gain[None, None, :, :]
    )
    product_table = product_table.reshape(-1, product_table.shape[-1])
    return product_table / jnp.sum(product_table, axis=1, keepdims=True)


def onehot_rows(dataset_tag, charge_tag, spin_tag, charge_count, spin_count, row_total):
    tag_rows = (dataset_tag * charge_count + charge_tag) * spin_count + spin_tag
    return (tag_rows[:, None] == jnp.arange(row_total, dtype=jnp.int32)[None, :]).astype(
        jnp.float32
    )


def select_rows(node_rows, slot_ids):
    atom_ids = lax.broadcasted_iota(jnp.int32, (1, node_rows.shape[0]), 1)
    selector = (slot_ids[:, None] == atom_ids).astype(jnp.bfloat16)
    return jnp.dot(selector, node_rows, preferred_element_type=jnp.float32)


def system_product(items):
    feat_rows, cot_rows, length_row, atoms_here, edges_here, source_row, target_row = items
    atom_slots = feat_rows.shape[0]
    edge_input = (select_rows(feat_rows, source_row) * envelope(length_row)[:, None]).astype(
        jnp.bfloat16
    )
    slot_index = lax.broadcasted_iota(jnp.int32, source_row.shape, 0)
    live_mask = (slot_index < edges_here).astype(jnp.float32)
    factor = live_mask * (float(atom_slots) / atoms_here.astype(jnp.float32))
    edge_grad = (select_rows(cot_rows, target_row) * factor[:, None]).astype(jnp.bfloat16)
    return lax.dot_general(
        edge_input, edge_grad, (((0,), (0,)), ((), ())), preferred_element_type=jnp.float32
    )


def adam_update(gradients, params, moment_one, moment_two, square_sum, norm_limit):
    clip_factor = jnp.minimum(1.0, norm_limit / (jnp.sqrt(square_sum) + 1e-06))
    clipped = clip_factor * gradients
    new_one = beta_one * moment_one + (1.0 - beta_one) * clipped
    new_two = beta_two * moment_two + (1.0 - beta_two) * clipped * clipped
    first_fix = 1.0 - beta_one**STEP
    second_fix = 1.0 - beta_two**STEP
    direction = new_one / first_fix / (jnp.sqrt(new_two / second_fix) + adam_eps)
    new_params = params - learn_rate * (direction + decay_rate * params)
    return (new_params, new_one, new_two)


def plain_local(
    node_feat,
    node_cot,
    edge_length,
    atom_count,
    edge_count,
    edge_source,
    edge_target,
    dataset_tag,
    charge_tag,
    spin_tag,
    dataset_gain,
    charge_gain,
    spin_gain,
    params,
    moment_one,
    moment_two,
):
    channels = node_feat.shape[2] // 2
    mixing = mixing_table(dataset_gain, charge_gain, spin_gain)
    tag_onehot = onehot_rows(
        dataset_tag, charge_tag, spin_tag, charge_gain.shape[0], spin_gain.shape[0], mixing.shape[0]
    )
    products = lax.map(
        system_product,
        (node_feat, node_cot, edge_length, atom_count, edge_count, edge_source, edge_target),
    )
    real_part = products[:, :channels, :channels] + products[:, channels:, channels:]
    imag_part = products[:, :channels, channels:] - products[:, channels:, :channels]
    system_grad = jnp.stack([real_part, imag_part], axis=2)
    local_term = jnp.einsum(
        "sk,scto->ckto", tag_onehot, system_grad, precision=lax.Precision.HIGHEST
    )
    summed = lax.psum_scatter(local_term, "shard", scatter_dimension=0, tiled=True)
    summed = lax.psum(summed, "rep")
    gradients = jnp.einsum("ke,ckto->ecto", mixing, summed, precision=lax.Precision.HIGHEST)
    square_sum = lax.psum(jnp.sum(gradients * gradients), "shard")
    norm_limit = math.sqrt(mixing.shape[1] * 2 * channels * channels)
    new_params, new_one, new_two = adam_update(
        gradients, params, moment_one, moment_two, square_sum, norm_limit
    )
    full_weights = lax.all_gather(new_params.astype(jnp.bfloat16), "shard", axis=1, tiled=True)
    return (new_params, new_one, new_two, full_weights)


MIB = 1024 * 1024
MESH = pl.DeviceIdType.MESH


def split_dot(left, right, contract):
    high = right.astype(jnp.bfloat16)
    low = (right - high.astype(jnp.float32)).astype(jnp.bfloat16)
    dims = (contract, ((), ()))
    return lax.dot_general(
        left, high, dims, preferred_element_type=jnp.float32
    ) + lax.dot_general(left, low, dims, preferred_element_type=jnp.float32)


def split_dot_left(left, right):
    high = left.astype(jnp.bfloat16)
    low = (left - high.astype(jnp.float32)).astype(jnp.bfloat16)
    dims = (((0,), (0,)), ((), ()))
    return lax.dot_general(
        high, right, dims, preferred_element_type=jnp.float32
    ) + lax.dot_general(low, right, dims, preferred_element_type=jnp.float32)


def expert_rows(mixing, summed, expert):
    total = mixing[0, expert] * summed[:, 0]
    for k in range(1, summed.shape[1]):
        total = total + mixing[k, expert] * summed[:, k]
    return total


def adam_rows(gradient, clip, params, moment_one, moment_two):
    clipped = clip * gradient
    new_one = beta_one * moment_one + (1.0 - beta_one) * clipped
    new_two = beta_two * moment_two + (1.0 - beta_two) * clipped * clipped
    first_fix = 1.0 - beta_one**STEP
    second_fix = 1.0 - beta_two**STEP
    direction = new_one / first_fix / (jnp.sqrt(new_two / second_fix) + adam_eps)
    return params - learn_rate * (direction + decay_rate * params), new_one, new_two


def system_sums(feat, cot, weight, source, target, atoms, edges, products):
    systems, slots, width = feat.shape
    channels = width // 2
    lanes = source.shape[1]

    def selectors(s):
        slot_index = lax.broadcasted_iota(jnp.int32, (1, lanes), 1)
        atom_index = lax.broadcasted_iota(jnp.int32, (slots, lanes), 0)
        count = jnp.full((1, lanes), atoms[s], jnp.int32).astype(jnp.float32)
        factor = jnp.where(slot_index < edges[s], float(slots) / count, 0.0)
        row = weight[pl.ds(s, 1), :] * factor
        left = jnp.where(atom_index == source[pl.ds(s, 1), :], row, 0.0).astype(jnp.bfloat16)
        right = jnp.where(atom_index == target[pl.ds(s, 1), :], 1.0, 0.0).astype(jnp.bfloat16)
        return left, right

    def system_product(s, pairs):
        mixed = split_dot_left(pairs, cot[s])
        real, imag = mixed[:, :channels], mixed[:, channels:]
        block = jnp.concatenate(
            [
                jnp.concatenate([real, imag], axis=1),
                jnp.concatenate([imag, -real], axis=1),
            ],
            axis=0,
        )
        rows = feat[s]
        stacked = jnp.concatenate([rows[:, :channels], rows[:, channels:]], axis=0)
        product = split_dot(stacked, block, ((0,), (0,)))
        products[s, pl.ds(0, channels, stride=2), :] = product[:, :channels]
        products[s, pl.ds(1, channels, stride=2), :] = product[:, channels:]

    def some_systems(i, carry):
        chosen = [selectors(i * STACKED + n) for n in range(STACKED)]
        left = jnp.concatenate([c[0] for c in chosen], axis=0)
        right = jnp.concatenate([c[1] for c in chosen], axis=0)
        pairs = lax.dot_general(
            right, left, (((1,), (1,)), ((), ())), preferred_element_type=jnp.float32
        )
        for n in range(STACKED):
            own = slice(n * slots, (n + 1) * slots)
            system_product(i * STACKED + n, pairs[own, own])
        return carry

    lax.fori_loop(0, systems // STACKED, some_systems, 0, unroll=2)


STACKED = 2
CROSS_PARTS = 2


def whole_kernel(
    shards, reps, norm_limit,
    feat_in, cot_in, length_in, atoms_in, edges_in, source_in, target_in,
    dataset_in, charge_in, spin_in, dataset_gain_in, charge_gain_in, spin_gain_in,
    params_in, one_in, two_in,
    new_params_out, new_one_out, new_two_out, weights,
    feat, cot, length, source, target, dataset_gain, charge_gain, spin_gain,
    params, moment_one, moment_two, new_params, new_one, new_two, table, atoms, edges, dataset, charge, spin, mixing,
    products, pieces, pair_in, pair_sum, slices, z_sum, z_in, summed, norms,
    fetch_sem, store_sem, table_sem, pair_sem, slice_send, slice_recv, ahead_send, ahead_recv, rep_send, rep_recv,
    norm_send, norm_recv, z_send, z_recv, y_send, y_recv, x_send, x_recv, core_send, core_recv,
):
    shard, rep = lax.axis_index("shard"), lax.axis_index("rep")
    planes, depth = reps // 2, shards // 2
    x, core = rep // 2, rep % 2
    z, y = shard // 2, shard % 2
    devices = shards * reps
    me = shard * reps + rep
    experts = params.shape[0]
    tags = summed.shape[1]

    fetches = [
        pltpu.make_async_copy(src, dst, fetch_sem.at[i])
        for i, (src, dst) in enumerate(
            (
                (source_in, source), (target_in, target), (length_in, length),
                (atoms_in, atoms), (edges_in, edges), (cot_in, cot), (feat_in, feat),
                (dataset_in, dataset), (charge_in, charge), (spin_in, spin),
                (dataset_gain_in, dataset_gain), (charge_gain_in, charge_gain),
                (spin_gain_in, spin_gain),
                (params_in, params), (one_in, moment_one), (two_in, moment_two),
            )
        )
    ]
    for fetch in fetches:
        fetch.start()

    barrier = pltpu.get_barrier_semaphore()
    for j in range(1, devices):
        other = lax.rem(me + j, devices)
        pl.semaphore_signal(
            barrier, inc=1, device_id=(other // reps, lax.rem(other, reps)), device_id_type=MESH
        )

    for fetch in fetches[:13]:
        fetch.wait()
    charges, spins = charge_gain.shape[0], spin_gain.shape[0]
    table[...] = jnp.zeros_like(table)
    for k in range(tags):
        d, c, s = k // (charges * spins), (k // spins) % charges, k % spins
        line = dataset_gain[d : d + 1, :] * charge_gain[c : c + 1, :] * spin_gain[s : s + 1, :]
        table[k : k + 1, 0:experts] = line / jnp.sum(line, axis=1, keepdims=True)
    to_scalars = pltpu.make_async_copy(table, mixing, table_sem)
    to_scalars.start()

    length[...] = envelope(length[...])
    system_sums(feat, cot, length, source, target, atoms, edges, products)

    systems, _, channels = products.shape
    rows_of = [
        (dataset[s] * charges + charge[s]) * spins + spin[s] for s in range(systems)
    ]
    takes = [
        [jnp.where(rows_of[s] == k, 1.0, 0.0) for s in range(systems)] for k in range(tags)
    ]

    block_rows = reps * 8

    def group(owner):
        at = pl.multiple_of(owner * block_rows, block_rows)
        terms = [products[s, pl.ds(at, block_rows), :] for s in range(systems)]
        for k in range(tags):
            total = takes[k][0] * terms[0]
            for s in range(1, systems):
                total = total + takes[k][s] * terms[s]
            for r in range(reps):
                pieces[r % 2, r // 2, owner, 8 * k : 8 * k + 8, :] = total[8 * r : 8 * r + 8, :]

    pl.semaphore_wait(barrier, devices - 1)

    def send(src, dst, send_sem, recv_sem, to):
        copy = pltpu.make_async_remote_copy(
            src_ref=src, dst_ref=dst, send_sem=send_sem, recv_sem=recv_sem,
            device_id=to, device_id_type=MESH,
        )
        copy.start()
        return copy

    sibling = (shard, x * 2 + 1 - core)
    started = []

    parts = [(dz, lax.rem(z + dz, depth)) for dz in [*range(1, depth), 0]]
    sides = [(dx, dy) for dx in range(planes) for dy in range(2) if (dx, dy) != (0, 0)]
    pair, sided, ahead = {}, {}, []
    for dz, to_z in parts:
        both = pl.ds(pl.multiple_of(to_z * 2, 2), 2)
        group(to_z * 2)
        group(to_z * 2 + 1)
        pair[dz] = send(
            pieces.at[1 - core, :, both], pair_in.at[:, both],
            pair_sem.at[0, dz], pair_sem.at[1, dz], sibling,
        )
    for dz, to_z in parts:
        both = pl.ds(pl.multiple_of(to_z * 2, 2), 2)
        pair[dz].wait_recv()
        pair_sum[:, both] = pieces[core, :, both] + pair_in[:, both]
        for n, (dx, dy) in enumerate(sides):
            to_x, to_y = lax.rem(x + dx, planes), lax.rem(y + dy, 2)
            sided[dz, n] = send(
                pair_sum.at[to_x, to_z * 2 + to_y], slices.at[dz, n],
                slice_send.at[dz, n], slice_recv.at[dz, n],
                (z * 2 + to_y, to_x * 2 + core),
            )
    for dz, to_z in parts:
        total = pair_sum[x, to_z * 2 + y]
        for n in range(len(sides)):
            sided[dz, n].wait_recv()
            total = total + slices[dz, n]
        if dz > 0:
            z_sum[dz] = total
            ahead.append(
                send(
                    z_sum.at[dz], z_in.at[dz], ahead_send.at[dz], ahead_recv.at[dz],
                    (to_z * 2 + y, rep),
                )
            )
    to_scalars.wait()
    for n, copy in enumerate(ahead):
        copy.wait_recv()
        total = total + z_in[n + 1]
    started += [*pair.values(), *sided.values(), *ahead]
    own = total.reshape(tags, 8, total.shape[-1])
    summed[rep] = own

    shared = []
    for j in range(1, reps):
        shared.append(
            send(
                summed.at[rep], summed.at[rep], rep_send.at[j], rep_recv.at[j],
                (shard, lax.rem(rep + j, reps)),
            )
        )
    squares = jnp.zeros(own.shape[1:], jnp.float32)
    for e in range(experts):
        gradient = expert_rows(mixing, own[None], e)[0]
        squares = squares + gradient * gradient
    norms[me] = squares
    normed = []
    for j in range(1, devices):
        other = lax.rem(me + j, devices)
        normed.append(
            send(
                norms.at[me], norms.at[me], norm_send.at[j], norm_recv.at[j],
                (other // reps, lax.rem(other, reps)),
            )
        )
    for fetch in fetches[13:]:
        fetch.wait()
    for copy in shared:
        copy.wait_recv()
    for copy in normed:
        copy.wait_recv()
    started += shared + normed
    square_sum = jnp.sum(jnp.sum(norms[...], axis=0), axis=(0, 1), keepdims=True)
    clip = jnp.minimum(1.0, norm_limit / (jnp.sqrt(square_sum) + 1e-06))

    half = experts // 2
    span = (half * 5) // 8
    cross = half - span
    first = core * half + x * cross
    part = cross // CROSS_PARTS
    chunks = [
        (core * half + x * span + n * part, part, True) for n in range(CROSS_PARTS)
    ] + [(core * half + cross, span - cross, False)]
    cross_other = core * half + (1 - x) * span
    rows = weights.shape[1] // shards

    def update(begin):
        def one(i, carry):
            e = lax.rem(begin + i, experts)
            new_params[e], new_one[e], new_two[e] = adam_rows(
                expert_rows(mixing, summed, e), clip, params[e], moment_one[e], moment_two[e]
            )
            weights[e, pl.ds(pl.multiple_of(shard * rows, rows), rows), :] = (
                new_params[e].reshape(rows, weights.shape[-1]).astype(jnp.bfloat16)
            )
            return carry

        return one

    def pass_on(begin, count, owner, send_sem, recv_sem, to):
        block = weights.at[
            pl.ds(begin, count), pl.ds(pl.multiple_of(owner * rows, rows), rows), :
        ]
        copy = send(block, block, send_sem, recv_sem, to)
        started.append(copy)
        return copy

    beside = (z * 2 + 1 - y, rep)
    across = (shard, (1 - x) * 2 + core)
    along = [[None] * depth for _ in chunks]
    turned = [[None] * depth for _ in chunks]
    for n, (begin, count, _) in enumerate(chunks):
        lax.fori_loop(0, count, update(begin), 0, unroll=count)
        for d in range(1, depth):
            to = lax.rem(z + d, depth) * 2 + y
            along[n][d] = pass_on(
                begin, count, shard, z_send.at[n, d], z_recv.at[n, d], (to, rep)
            )
        turned[n][0] = pass_on(begin, count, shard, y_send.at[n, 0], y_recv.at[n, 0], beside)
    lax.fori_loop(0, experts - span, update(first + span), 0, unroll=2)
    stores = [
        pltpu.make_async_copy(src, dst, store_sem.at[i])
        for i, (src, dst) in enumerate(
            ((new_params, new_params_out), (new_one, new_one_out), (new_two, new_two_out))
        )
    ]
    for store in stores:
        store.start()

    crossed, paired = [[] for _ in range(shards)], []
    last = len(chunks) - 1

    def arrived(n, slot, owner):
        begin, count, crosses = chunks[n]
        if crosses:
            copy = pass_on(begin, count, owner, x_send.at[n, slot], x_recv.at[n, slot], across)
            crossed[slot].append(copy)
        if n == last:
            paired.append(
                pass_on(first, span, owner, core_send.at[0, slot], core_recv.at[0, slot], sibling)
            )

    def from_across(slot, owner):
        for copy in crossed[slot]:
            copy.wait_recv()
        paired.append(
            pass_on(
                cross_other, cross, owner, core_send.at[1, slot], core_recv.at[1, slot], sibling
            )
        )

    def owner_at(d, side):
        return lax.rem(z + depth - d, depth) * 2 + (y if side == 0 else 1 - y)

    def turned_in(n):
        for d in range(1, depth):
            turned[n][d].wait_recv()
            arrived(n, depth + d, owner_at(d, 1))

    for n, (begin, count, _) in enumerate(chunks):
        turned[n][0].wait_recv()
        arrived(n, depth, owner_at(0, 1))
        for d in range(1, depth):
            along[n][d].wait_recv()
            turned[n][d] = pass_on(
                begin, count, owner_at(d, 0), y_send.at[n, d], y_recv.at[n, d], beside
            )
            arrived(n, d, owner_at(d, 0))
        if n > 0:
            turned_in(n - 1)
    from_across(depth, owner_at(0, 1))
    for d in range(1, depth):
        from_across(d, owner_at(d, 0))
    turned_in(last)
    for d in range(1, depth):
        from_across(depth + d, owner_at(d, 1))
    for copy in paired:
        copy.wait_recv()
    for copy in started:
        copy.wait_send()
    for store in stores:
        store.wait()


def finish_kernel(*refs):
    count = (len(refs) - 2) // 3
    load_sem, store_sem = refs[-2:]
    loads, stores = [], []
    for i in range(count):
        source, result, held = refs[i], refs[count + i], refs[2 * count + i]
        rows = source.shape[0] // FINISH_PARTS
        for n in range(FINISH_PARTS):
            block = pl.ds(n * rows, rows)
            loads.append(
                pltpu.make_async_copy(source.at[block], held.at[block], load_sem.at[i, n])
            )
            stores.append(
                pltpu.make_async_copy(held.at[block], result.at[block], store_sem.at[i, n])
            )
    for load in loads:
        load.start()
    for load, store in zip(loads, stores):
        load.wait()
        store.start()
    for store in stores:
        store.wait()


FINISH_PARTS = 4


def kernel_local(shards, reps, *args):
    params = args[13]
    experts, own_channels, parts, channels = params.shape
    planes, depth, devices = reps // 2, shards // 2, shards * reps
    f32, bf16, i32 = jnp.float32, jnp.bfloat16, jnp.int32
    dma = pltpu.SemaphoreType.DMA
    anywhere = pl.BlockSpec(memory_space=pl.ANY)
    vmem = pl.BlockSpec(memory_space=pltpu.VMEM)
    systems, lanes = args[2].shape
    gains = args[10:13]
    tags = gains[0].shape[0] * gains[1].shape[0] * gains[2].shape[0]
    slice_rows = tags * 8
    rows = own_channels * parts
    states = [a.reshape(experts, reps, 8, channels) for a in args[13:16]]
    state = (experts, reps, 8, channels)
    norm_limit = math.sqrt(experts * parts * channels * channels)
    chunk_total = CROSS_PARTS + 1

    def held(array):
        return pltpu.VMEM(array.shape, array.dtype)

    def pairs(*shape):
        return [dma(shape), dma(shape)]

    outs = [jax.ShapeDtypeStruct(state, f32)] * 3
    outs.append(jax.ShapeDtypeStruct((experts, shards * rows, channels), bf16))
    results = pl.pallas_call(
        functools.partial(whole_kernel, shards, reps, norm_limit),
        out_shape=outs,
        in_specs=[anywhere] * 16,
        out_specs=[anywhere] * 3 + [vmem],
        scratch_shapes=[
            held(args[0]), held(args[1]), held(args[2]), held(args[5]), held(args[6]),
            *[held(a) for a in gains],
            *[pltpu.VMEM(state, f32)] * 6,
            pltpu.VMEM((tags, 128), f32),
            *[pltpu.SMEM((systems,), i32)] * 5,
            pltpu.SMEM((tags, 128), f32),
            pltpu.VMEM((systems, channels * parts, channels), f32),
            pltpu.VMEM((2, planes, shards, slice_rows, channels), f32),
            pltpu.VMEM((planes, shards, slice_rows, channels), f32),
            pltpu.VMEM((planes, shards, slice_rows, channels), f32),
            pltpu.VMEM((depth, planes * 2 - 1, slice_rows, channels), f32),
            pltpu.VMEM((depth, slice_rows, channels), f32),
            pltpu.VMEM((depth, slice_rows, channels), f32),
            pltpu.VMEM((reps, tags, 8, channels), f32),
            pltpu.VMEM((devices, 8, channels), f32),
            dma((16,)),
            dma((3,)),
            dma,
            dma((2, depth)),
            *pairs(depth, planes * 2 - 1),
            *pairs(depth),
            *pairs(reps),
            *pairs(devices),
            *pairs(chunk_total, depth),
            *pairs(chunk_total, depth),
            *pairs(CROSS_PARTS, shards),
            *pairs(2, shards),
        ],
        compiler_params=pltpu.CompilerParams(
            collective_id=0, has_side_effects=True, vmem_limit_bytes=60 * MIB
        ),
        name="whole",
    )(*args[:13], *states)

    outs = pl.pallas_call(
        finish_kernel,
        out_shape=outs,
        in_specs=[anywhere] * 4,
        out_specs=[anywhere] * 4,
        scratch_shapes=[*[held(a) for a in outs], *pairs(4, FINISH_PARTS)],
        compiler_params=pltpu.CompilerParams(vmem_limit_bytes=60 * MIB),
        name="finish",
    )(*results)
    local_states = [a.reshape(params.shape) for a in outs[:3]]
    return (*local_states, outs[3].reshape(experts, shards * own_channels, parts, channels))


def solution(mesh):
    placed = (
        P(("shard", "rep"), None, None),
        P(("shard", "rep"), None, None),
        P(("shard", "rep"), None),
        P(("shard", "rep")),
        P(("shard", "rep")),
        P(("shard", "rep"), None),
        P(("shard", "rep"), None),
        P(("shard", "rep")),
        P(("shard", "rep")),
        P(("shard", "rep")),
        P(),
        P(),
        P(),
        P(None, "shard", None, None),
        P(None, "shard", None, None),
        P(None, "shard", None, None),
    )
    shards, reps = mesh.shape["shard"], mesh.shape["rep"]

    def local(*args):
        params = args[13]
        even = shards % 2 == 0 and args[2].shape[0] % STACKED == 0
        if reps == 4 and even and params.shape[1] * params.shape[2] == 8 * reps:
            return kernel_local(shards, reps, *args)
        return plain_local(*args)

    return jax.shard_map(
        local,
        mesh=mesh,
        in_specs=placed,
        out_specs=(
            P(None, "shard", None, None),
            P(None, "shard", None, None),
            P(None, "shard", None, None),
            P(),
        ),
        check_vma=False,
    )
```
